256 devices in a mesh: rows: 32 (over x, y, z_lo), cols: 8 (over z_hi, core).
Axes of the slice: x: 4, y: 4, z: 8 (z_hi: 4, z_lo: 2; z = z_hi * 2 + z_lo), core: 2. Of those that a mesh axis runs over, the one named last changes fastest.
Arguments:
- hidden_in: bfloat16 [24576, 1024], P('rows'), may hold values from -6 to 6
- w_out: bfloat16 [1024, 4096], P('rows'), may hold values from -0.1875 to 0.1875
- inv_factor: float32 [4096, 4096], P('rows'), as said below
- treat_feat: bfloat16 [24576, 1024], P('rows', 'cols'), may hold values from -6 to 6
- section_cot: bfloat16 [24576, 1024], P('rows', 'cols'), may hold values from -6 to 6
Outputs:
- grad_w: float32 [1024, 4096], P('rows', 'cols')
The draws below stay inside these ranges and needn't reach their ends.
Inputs may be any that keep to these rules, and one draw needn't show every extreme that they name: inv_factor is lower triangular with a positive diagonal.
All inputs are finite; a program needn't handle non-finite values.
Results may differ from the reference program's by a relative error of at most 0.023.
Values may be sent and summed in bfloat16 or wider, within the bound.
No kernel may reach another device: no remote copies, remote signals or barrier semaphores. Data moves between devices by JAX's collectives and lax.ppermute only.
A program may use at most 128 MiB of HBM per device.

```python
import jax
import jax.numpy as jnp
from jax import lax

HID = 1024
FEAT = 4096
TREAT = 1024
ROWS = 24576
N_COLS = 8


def draw_inv_factor(key, part):
    key_diag, key_off = jax.random.split(jax.random.fold_in(key, 17))
    row_ids = jnp.arange(FEAT, dtype=jnp.int32)[:, None]
    col_ids = jnp.arange(FEAT, dtype=jnp.int32)[None, :]
    diag_vals = jnp.exp(jax.random.uniform(key_diag, (FEAT, 1), jnp.float32, jnp.log(0.5), jnp.log(2.0)))
    off_vals = jnp.clip(jax.random.normal(key_off, (FEAT, FEAT), jnp.float32), -6.0, 6.0)
    off_vals = off_vals * (0.5 / jnp.sqrt(jnp.float32(FEAT)))
    lower = jnp.where(col_ids < row_ids, off_vals, 0.0)
    lower = lower + jnp.where(col_ids == row_ids, diag_vals, 0.0)
    scale = (120.0 * jnp.sqrt(jnp.float32(ROWS))) ** (-0.5)
    return (lower * scale).astype(jnp.float32)


def with_spikes(array, rng, source, target, parts, factor):
    owner, partner = [(jnp.arange(array.shape[position]) // (array.shape[position] // parts)).reshape([-1 if axis == position else 1 for axis in range(array.ndim)]) for position in (source, target)]
    chosen = jax.random.permutation(rng, parts)[partner]
    strong = (owner == chosen) | (owner == (partner + parts // 2) % parts)
    return jnp.where(strong, factor * array, array)


def level_of(rng, extent, pieces, smallest, top_value):
    def one(position, blocks):
        heights = jax.random.uniform(jax.random.fold_in(jax.random.fold_in(rng, 6), position), (blocks,), jnp.float32, smallest / len(pieces), top_value / len(pieces))
        return jnp.repeat(jnp.exp(heights), extent[position] // blocks).reshape((-1,) + (1,) * (len(extent) - position - 1))

    gain = one(*pieces[0])
    for cut in pieces[1:]:
        gain = gain * one(*cut)
    return gain


def gaussian(key, shape, spread, reach, shards=(), kind=jnp.bfloat16):
    result = spread * jax.random.normal(key, shape, jnp.float32)
    if shards:
        result = result * level_of(key, shape, shards, -0.22, 0.18)
    return jnp.clip(result, -reach, reach).astype(kind)


def heavy_noise(own_key, dims, spread, limit, cuts, heavy, kind=jnp.bfloat16):
    array = spread * jax.random.normal(own_key, dims, jnp.float32)
    if cuts:
        array = array * level_of(own_key, dims, cuts, -0.22, 0.18)
    return jnp.clip(with_spikes(array, jax.random.fold_in(own_key, 3), *heavy), -limit, limit).astype(kind)


def setup_inputs(seed: int = 0) -> dict:
    arg_keys = jax.random.split(jax.random.key(seed), 6)
    hidden_in = heavy_noise(arg_keys[0], (ROWS, HID), 1.0, 6.0, ((0, 32),), (0, 1, 32, 2.75))
    w_out = gaussian(arg_keys[1], (HID, FEAT), HID ** -0.5, 0.1875, ((0, 32),))
    inv_factor = draw_inv_factor(jax.random.fold_in(arg_keys[5], 71), 0)
    treat_feat = gaussian(arg_keys[3], (ROWS, TREAT), 1.0, 6.0, ((0, 32), (1, 8)))
    section_cot = gaussian(arg_keys[4], (ROWS, TREAT), 1.0, 6.0, ((0, 32), (1, 8)))
    return {"hidden_in": hidden_in, "w_out": w_out, "inv_factor": inv_factor, "treat_feat": treat_feat, "section_cot": section_cot}


def reference(hidden_in, w_out, inv_factor, treat_feat, section_cot):
    pre = jnp.dot(hidden_in, w_out, preferred_element_type=jnp.float32)
    psi = jax.nn.silu(pre).astype(jnp.bfloat16)
    b_phi = jnp.dot(psi.T, treat_feat, preferred_element_type=jnp.float32)
    b_cot = jnp.dot(psi.T, section_cot, preferred_element_type=jnp.float32)
    stacked = jnp.concatenate([b_phi, b_cot], axis=1)
    middle = jnp.dot(inv_factor, stacked, precision=lax.Precision.HIGHEST, preferred_element_type=jnp.float32)
    solved = jnp.dot(inv_factor.T, middle, precision=lax.Precision.HIGHEST, preferred_element_type=jnp.float32)
    solved = solved.astype(jnp.bfloat16)
    sol_v = solved[:, :TREAT]
    sol_m = solved[:, TREAT:]
    fit_r = jnp.dot(psi, sol_v, preferred_element_type=jnp.float32)
    fit_s = jnp.dot(psi, sol_m, preferred_element_type=jnp.float32)
    u_cot = (section_cot - fit_s).astype(jnp.bfloat16)
    u_phi = (treat_feat - fit_r).astype(jnp.bfloat16)
    width = TREAT // N_COLS
    dpsi = jnp.zeros(pre.shape, jnp.float32)
    for group in range(N_COLS):
        lo = group * width
        left = jnp.concatenate([u_cot[:, lo:lo + width], u_phi[:, lo:lo + width]], axis=1)
        right = jnp.concatenate([sol_v[:, lo:lo + width], sol_m[:, lo:lo + width]], axis=1)
        term = jnp.dot(left, right.T, preferred_element_type=jnp.float32).astype(jnp.bfloat16)
        term = lax.optimization_barrier(term)
        dpsi = dpsi + term.astype(jnp.float32)
    sig = jax.nn.sigmoid(pre)
    dpre = (dpsi * sig * (1.0 + pre * (1.0 - sig))).astype(jnp.bfloat16)
    grad_w = jnp.dot(hidden_in.T, dpre, preferred_element_type=jnp.float32)
    return grad_w * (1.0 / jnp.sqrt(jnp.float32(ROWS)))
```

```python
import jax
import jax.numpy as jnp
from jax import lax
from jax.sharding import PartitionSpec as P

NX, NY, NZ, NH, NC = 4, 4, 2, 4, 2
BF = jnp.bfloat16
F32 = jnp.float32


def row_id(x, y, z):
    return (x % NX) * (NY * NZ) + (y % NY) * NZ + (z % NZ)


def get_rows(value, dx=0, dy=0, dz=0):
    pairs = [
        (row_id(x + dx, y + dy, z + dz), row_id(x, y, z))
        for x in range(NX)
        for y in range(NY)
        for z in range(NZ)
    ]
    return lax.ppermute(value, "rows", pairs)


def get_x(value, k):
    return get_rows(value, dx=k)


def get_y(value, k):
    return get_rows(value, dy=k)


def get_z(value):
    return get_rows(value, dz=1)


def get_cols(value, dh=0, dc=0):
    pairs = [
        (((h + dh) % NH) * NC + (c + dc) % NC, h * NC + c) for h in range(NH) for c in range(NC)
    ]
    return lax.ppermute(value, "cols", pairs)


def dot(a, b, contract=((1,), (0,))):
    return lax.dot_general(a, b, (contract, ((), ())), preferred_element_type=F32)


def pick(natural, size):
    j = lax.broadcasted_iota(jnp.int32, (size, size), 1)
    k = lax.broadcasted_iota(jnp.int32, (size, size), 0)
    return jnp.where(k == natural(j), 1.0, 0.0).astype(BF)


def ring_gather(block, get):
    half = block.shape[0] // 2
    one = get(block, 1)
    three = get(block, 3)
    two_a = get(one[:half], 1)
    two_b = get(three[half:], 3)
    return jnp.concatenate([block, one, two_a, two_b, three], axis=0)


def direct_gather(block, get):
    return jnp.concatenate([block] + [get(block, k) for k in (1, 2, 3)], axis=0)


def direct_reduce(parts, get):
    sent = parts.astype(BF)
    total = parts[0]
    for k in (1, 2, 3):
        total = total + get(sent[(4 - k) % 4], k).astype(F32)
    return total


def silu(v):
    return (0.5 * v) * (1.0 + jnp.tanh(0.5 * v))


def shards(hidden_in, w_out, inv_factor, treat_feat, section_cot):
    n_here = hidden_in.shape[0]
    row_total = n_here * lax.axis_size("rows")
    r = lax.axis_index("rows")
    c = lax.axis_index("cols")
    x, y, z = r // (NY * NZ), (r // NZ) % NY, r % NZ
    h, core = c // NC, c % NC

    w_half = lax.dynamic_index_in_dim(w_out.reshape(32, NH, NC, 512), core, 2, keepdims=False)
    w_half = w_half.reshape(32, NH, 2, 256).transpose(2, 0, 1, 3).reshape(2, 32, 1024)
    w_pair = jnp.concatenate([w_half, get_z(w_half)], axis=1)
    w_a = direct_gather(w_pair[0], get_x)
    w_b = direct_gather(w_pair[1], get_y)
    w_a = ring_gather(w_a, get_y)
    w_b = ring_gather(w_b, get_x)

    def natural_a(j):
        ys, xs, zs, i = j // 256, (j // 64) % 4, (j // 32) % 2, j % 32
        return ((x + xs) % 4) * 256 + ((y + ys) % 4) * 64 + ((z + zs) % 2) * 32 + i

    def natural_b(j):
        xs, ys, zs, i = j // 256, (j // 64) % 4, (j // 32) % 2, j % 32
        return ((x + xs) % 4) * 256 + ((y + ys) % 4) * 64 + ((z + zs) % 2) * 32 + i

    h_a = dot(hidden_in, pick(natural_a, 1024)).astype(BF)
    h_b = dot(hidden_in, pick(natural_b, 1024)).astype(BF)

    l_half = lax.dynamic_slice_in_dim(inv_factor, core * 64, 64, 0).astype(BF)
    l_half = l_half.reshape(64, NH * NC, NY, 128)

    def l_cols(k):
        return lax.dynamic_index_in_dim(l_half, (y + 4 - k) % 4, 2, keepdims=False).reshape(64, 1024)

    l_parts = jnp.stack([l_cols(0)] + [get_y(l_cols(k), k) for k in (1, 2, 3)])
    l_parts = jnp.concatenate([l_parts, get_z(l_parts)], axis=1)
    l_block = jnp.concatenate([l_parts, get_cols(l_parts, dc=1)], axis=1).reshape(1024, 1024)

    def natural_l(j):
        xs, rc, hs, i = j // 256, (j // 128) % 2, (j // 32) % 4, j % 32
        return (hs * 2 + (core + rc) % 2) * 128 + ((x + xs) % 4) * 32 + i

    l_block = dot(l_block, pick(natural_l, 1024)).astype(BF)

    psi_a = silu(dot(h_a, w_a)).astype(BF)
    psi_a_other = get_cols(psi_a, dc=1)
    psi_b = silu(dot(h_b, w_b)).astype(BF)
    psi_b_other = get_cols(psi_b, dc=1)
    psis = [psi_a, psi_b, psi_a_other, psi_b_other]

    targets = jnp.concatenate([treat_feat, section_cot], axis=1)
    cross = [dot(p, targets, ((0,), (0,))).astype(BF) for p in psis]
    cross = jnp.stack(cross).reshape(2, 2, 4, 2, 4, 32, 2, 128)
    cross = cross.transpose(4, 1, 3, 6, 0, 2, 5, 7).reshape(32, 256, 128)
    cross = lax.all_to_all(cross, "rows", 0, 0, tiled=True)
    cross = jnp.sum(cross.astype(F32), axis=0).astype(BF)

    cross = direct_gather(cross, get_x)
    middle = dot(l_block, cross).reshape(4, 256, 128)
    middle = direct_reduce(middle, get_y).astype(BF)
    middle = direct_gather(middle, get_y)
    solved = dot(l_block, middle, ((0,), (0,))).reshape(4, 256, 128)
    solved = direct_reduce(solved, get_x).astype(BF)

    sol = lax.all_to_all(jnp.broadcast_to(solved[None], (32, 256, 128)), "rows", 0, 0, tiled=True)
    sol = sol.reshape(4, 2, 2, 2, 2, 4, 32, 128).transpose(4, 1, 5, 2, 0, 6, 3, 7).reshape(4, 1024, 256)

    own = solved.reshape(2, NH, 32, 128)
    own = jnp.where(core == 0, own, own[::-1]).transpose(1, 0, 2, 3).reshape(8, 32, 128)
    own = lax.all_to_all(own, "cols", 0, 0, tiled=True)

    fitted = dot(psis[0], sol[0])
    for k in (1, 2, 3):
        fitted = fitted + dot(psis[k], sol[k])
    width = treat_feat.shape[1]
    u_cot = (section_cot - fitted[:, width:]).astype(BF)
    u_phi = (treat_feat - fitted[:, :width]).astype(BF)
    u = jnp.concatenate([u_cot, u_phi], axis=1)

    u_one = get_cols(u, dh=1)
    u_three = get_cols(u, dh=3)
    sol2 = lax.all_to_all(jnp.broadcast_to(own[None], (32, 8, 32, 128)), "rows", 0, 0, tiled=True)
    sol2 = sol2.reshape(4, 4, 2, 8, 32, 128).transpose(3, 1, 0, 4, 2, 5).reshape(8, 512, 256)
    half = n_here // 2
    u_two_a = get_cols(u_one[:half], dh=1)
    u_two_b = get_cols(u_three[half:], dh=3)
    u_two = jnp.concatenate([u_two_a, u_two_b], axis=0)

    def term(value, dh):
        other = get_cols(value, dc=1)
        left = jnp.concatenate([value, other], axis=1)
        hs = (h + dh) % NH
        right = jnp.concatenate(
            [
                lax.dynamic_index_in_dim(sol2, hs * 2 + core, 0, keepdims=False),
                lax.dynamic_index_in_dim(sol2, hs * 2 + 1 - core, 0, keepdims=False),
            ],
            axis=1,
        )
        return dot(left, right, ((1,), (1,)))

    dpsi = term(u, 0) + term(u_one, 1) + term(u_three, 3) + term(u_two, 2)

    pre = jnp.concatenate(
        [
            dot(h_a, lax.dynamic_slice_in_dim(w_a, h * 256, 256, 1)),
            dot(h_b, lax.dynamic_slice_in_dim(w_b, h * 256, 256, 1)),
        ],
        axis=1,
    )
    sig = jax.nn.sigmoid(pre)
    dpre = (dpsi * (sig * (1.0 + pre * (1.0 - sig)))).astype(BF)
    grad = dot(hidden_in, dpre, ((0,), (0,))).astype(BF).reshape(32, 32, 512)
    grad = lax.all_to_all(grad, "rows", 0, 0, tiled=True)
    return jnp.sum(grad.astype(F32), axis=0) * (1.0 / jnp.sqrt(jnp.float32(row_total)))


def solution(mesh):
    placed = (
        P("rows", None),
        P("rows", None),
        P("rows", None),
        P("rows", "cols"),
        P("rows", "cols"),
    )
    return jax.shard_map(
        shards, mesh=mesh, in_specs=placed, out_specs=P("rows", "cols"), check_vma=False
    )
```

```python
import jax
import jax.numpy as jnp
from jax import lax
from jax.experimental import pallas as pl
from jax.experimental.pallas import tpu as pltpu
from jax.sharding import PartitionSpec as P

NX, NY, NZ, NH, NC = 4, 4, 2, 4, 2
BF = jnp.bfloat16
F32 = jnp.float32


def row_id(x, y, z):
    return (x % NX) * (NY * NZ) + (y % NY) * NZ + (z % NZ)


def get_rows(value, dx=0, dy=0, dz=0):
    pairs = [
        (row_id(x + dx, y + dy, z + dz), row_id(x, y, z))
        for x in range(NX)
        for y in range(NY)
        for z in range(NZ)
    ]
    return lax.ppermute(value, "rows", pairs)


def get_x(value, k):
    return get_rows(value, dx=k)


def get_y(value, k):
    return get_rows(value, dy=k)


def get_z(value):
    return get_rows(value, dz=1)


def get_cols(value, dh=0, dc=0):
    pairs = [
        (((h + dh) % NH) * NC + (c + dc) % NC, h * NC + c) for h in range(NH) for c in range(NC)
    ]
    return lax.ppermute(value, "cols", pairs)


def dot(a, b, contract=((1,), (0,))):
    return lax.dot_general(a, b, (contract, ((), ())), preferred_element_type=F32)


def pick(natural, size):
    j = lax.broadcasted_iota(jnp.int32, (size, size), 1)
    k = lax.broadcasted_iota(jnp.int32, (size, size), 0)
    return jnp.where(k == natural(j), 1.0, 0.0).astype(BF)


def ring_gather(block, get):
    half = block.shape[0] // 2
    one = get(block, 1)
    three = get(block, 3)
    two_a = get(one[:half], 1)
    two_b = get(three[half:], 3)
    return jnp.concatenate([block, one, two_a, two_b, three], axis=0)


def direct_gather(block, get):
    return jnp.concatenate([block] + [get(block, k) for k in (1, 2, 3)], axis=0)


def direct_reduce(parts, get):
    sent = parts.astype(BF)
    total = parts[0]
    for k in (1, 2, 3):
        total = total + get(sent[(4 - k) % 4], k).astype(F32)
    return total


def local_call(kernel, outs, args, scratch=(), flops=0):
    specs = [pl.BlockSpec(memory_space=pltpu.VMEM)] * len(args)
    size = sum(a.size * a.dtype.itemsize for a in args)
    return pl.pallas_call(
        kernel,
        out_shape=outs,
        in_specs=specs,
        out_specs=pl.BlockSpec(memory_space=pltpu.VMEM),
        scratch_shapes=list(scratch),
        compiler_params=pltpu.CompilerParams(vmem_limit_bytes=24 * 1024 * 1024),
        cost_estimate=pl.CostEstimate(flops=flops, bytes_accessed=size, transcendentals=0),
    )(*args)


def blocks():
    for k in range(4):
        for hs in range(NH):
            for ys in range(2):
                for xs in range(NX):
                    for zs in range(NZ):
                        dest = row_id(xs, (k % 2) * 2 + ys, zs)
                        yield k, hs * 256 + ys * 128 + xs * 32, zs, dest, (k // 2) * 128 + hs * 32


def cross_kernel(c0, c1, c2, c3, out):
    chunks = (c0, c1, c2, c3)
    for k, row, zs, dest, place in blocks():
        out[dest, place : place + 32, :] = chunks[k][row : row + 32, zs * 128 : (zs + 1) * 128]


def fit_kernel(p0, p1, p2, p3, sol, treat, cot, u, chunk, fitted):
    psis = (p0, p1, p2, p3)
    n = u.shape[0]
    tile = 256
    for k in range(4):
        for kk, row, zs, dest, place in blocks():
            if kk == k:
                chunk[row : row + 32, zs * 128 : (zs + 1) * 128] = sol[dest, place : place + 32, :]

        @pl.loop(0, n // tile)
        def _(i):
            rows = pl.ds(pl.multiple_of(i * tile, tile), tile)
            part = jnp.dot(psis[k][rows, :], chunk[...], preferred_element_type=F32)
            if k == 0:
                fitted[rows, :] = part
            elif k < 3:
                fitted[rows, :] += part
            else:
                part = fitted[rows, :] + part
                u[rows, 0:128] = (cot[rows, :].astype(F32) - part[:, 128:256]).astype(BF)
                u[rows, 128:256] = (treat[rows, :].astype(F32) - part[:, 0:128]).astype(BF)


def own_kernel(got, out):
    for k in range(8):
        for xs in range(NX):
            for ys in range(NY):
                for zs in range(NZ):
                    row = (ys * NX + xs) * 32
                    out[k, row : row + 32, zs * 128 : (zs + 1) * 128] = got[
                        row_id(xs, ys, zs), k
                    ]


def silu(v):
    return (0.5 * v) * (1.0 + jnp.tanh(0.5 * v))


def shards(hidden_in, w_out, inv_factor, treat_feat, section_cot):
    n_here = hidden_in.shape[0]
    row_total = n_here * lax.axis_size("rows")
    r = lax.axis_index("rows")
    c = lax.axis_index("cols")
    x, y, z = r // (NY * NZ), (r // NZ) % NY, r % NZ
    h, core = c // NC, c % NC

    w_half = lax.dynamic_index_in_dim(w_out.reshape(32, NH, NC, 512), core, 2, keepdims=False)
    w_half = w_half.reshape(32, NH, 2, 256).transpose(2, 0, 1, 3).reshape(2, 32, 1024)
    w_pair = jnp.concatenate([w_half, get_z(w_half)], axis=1)
    w_a = direct_gather(w_pair[0], get_x)
    w_b = direct_gather(w_pair[1], get_y)
    w_a = ring_gather(w_a, get_y)
    w_b = ring_gather(w_b, get_x)

    def natural_a(j):
        ys, xs, zs, i = j // 256, (j // 64) % 4, (j // 32) % 2, j % 32
        return ((x + xs) % 4) * 256 + ((y + ys) % 4) * 64 + ((z + zs) % 2) * 32 + i

    def natural_b(j):
        xs, ys, zs, i = j // 256, (j // 64) % 4, (j // 32) % 2, j % 32
        return ((x + xs) % 4) * 256 + ((y + ys) % 4) * 64 + ((z + zs) % 2) * 32 + i

    h_a = dot(hidden_in, pick(natural_a, 1024)).astype(BF)
    h_b = dot(hidden_in, pick(natural_b, 1024)).astype(BF)

    l_half = lax.dynamic_slice_in_dim(inv_factor, core * 64, 64, 0).astype(BF)
    l_half = l_half.reshape(64, NH * NC, NY, 128)

    def l_cols(k):
        return lax.dynamic_index_in_dim(l_half, (y + 4 - k) % 4, 2, keepdims=False).reshape(64, 1024)

    l_parts = jnp.stack([l_cols(0)] + [get_y(l_cols(k), k) for k in (1, 2, 3)])
    l_parts = jnp.concatenate([l_parts, get_z(l_parts)], axis=1)
    l_block = jnp.concatenate([l_parts, get_cols(l_parts, dc=1)], axis=1).reshape(1024, 1024)

    def natural_l(j):
        xs, rc, hs, i = j // 256, (j // 128) % 2, (j // 32) % 4, j % 32
        return (hs * 2 + (core + rc) % 2) * 128 + ((x + xs) % 4) * 32 + i

    l_block = dot(l_block, pick(natural_l, 1024)).astype(BF)

    w_a, w_b, l_block = lax.optimization_barrier((w_a, w_b, l_block))
    psi_a = silu(dot(h_a, w_a)).astype(BF)
    psi_a_other = get_cols(psi_a, dc=1)
    psi_b = silu(dot(h_b, w_b)).astype(BF)
    psi_b_other = get_cols(psi_b, dc=1)
    psis = [psi_a, psi_b, psi_a_other, psi_b_other]

    targets = jnp.concatenate([treat_feat, section_cot], axis=1)
    cross = [dot(p, targets, ((0,), (0,))).astype(BF) for p in psis]
    cross = local_call(cross_kernel, jax.ShapeDtypeStruct((32, 256, 128), BF), cross)
    cross = lax.all_to_all(cross, "rows", 0, 0, tiled=True)
    cross = jnp.sum(cross.astype(F32), axis=0).astype(BF)

    cross = direct_gather(cross, get_x)
    middle = dot(l_block, cross).reshape(4, 256, 128)
    middle = direct_reduce(middle, get_y).astype(BF)
    middle = direct_gather(middle, get_y)
    solved = dot(l_block, middle, ((0,), (0,))).reshape(4, 256, 128)
    solved = direct_reduce(solved, get_x).astype(BF)

    own = solved.reshape(2, NH, 32, 128)
    other = get_cols(own[1], dc=1)
    own = jnp.stack([own[0], other], axis=1)
    own = jnp.concatenate(
        [lax.dynamic_slice_in_dim(own, h, 1, 0)]
        + [get_cols(lax.dynamic_slice_in_dim(own, (h + 4 - k) % 4, 1, 0), dh=k) for k in (1, 2, 3)]
    ).reshape(8, 32, 128)

    sol = lax.all_to_all(jnp.broadcast_to(solved[None], (32, 256, 128)), "rows", 0, 0, tiled=True)
    sol, own = lax.optimization_barrier((sol, own))
    sol2 = lax.all_to_all(jnp.broadcast_to(own[None], (32, 8, 32, 128)), "rows", 0, 0, tiled=True)
    n_width = 2 * treat_feat.shape[1]
    u = local_call(
        fit_kernel,
        jax.ShapeDtypeStruct((n_here, n_width), BF),
        psis + [sol, treat_feat, section_cot],
        scratch=[pltpu.VMEM((1024, n_width), BF), pltpu.VMEM((n_here, n_width), F32)],
        flops=2 * n_here * 4096 * n_width,
    )

    u_one = get_cols(u, dh=1)
    u_three = get_cols(u, dh=3)
    sol2 = local_call(own_kernel, jax.ShapeDtypeStruct((8, 512, 256), BF), [sol2])
    half = n_here // 2
    u_two_a = get_cols(u_one[:half], dh=1)
    u_two_b = get_cols(u_three[half:], dh=3)
    u_two = jnp.concatenate([u_two_a, u_two_b], axis=0)

    def term(value, dh):
        other = get_cols(value, dc=1)
        left = jnp.concatenate([value, other], axis=1)
        right = jnp.concatenate([sol2[2 * dh], sol2[2 * dh + 1]], axis=1)
        return dot(left, right, ((1,), (1,)))

    dpsi = term(u, 0) + term(u_one, 1) + term(u_three, 3) + term(u_two, 2)

    pre = jnp.concatenate(
        [
            dot(h_a, lax.dynamic_slice_in_dim(w_a, h * 256, 256, 1)),
            dot(h_b, lax.dynamic_slice_in_dim(w_b, h * 256, 256, 1)),
        ],
        axis=1,
    )
    sig = jax.nn.sigmoid(pre)
    dpre = (dpsi * (sig * (1.0 + pre * (1.0 - sig)))).astype(BF)
    grad = dot(hidden_in, dpre, ((0,), (0,))).astype(BF).reshape(32, 32, 512)
    grad = lax.all_to_all(grad, "rows", 0, 0, tiled=True)
    return jnp.sum(grad.astype(F32), axis=0) * (1.0 / jnp.sqrt(jnp.float32(row_total)))


def solution(mesh):
    placed = (
        P("rows", None),
        P("rows", None),
        P("rows", None),
        P("rows", "cols"),
        P("rows", "cols"),
    )
    return jax.shard_map(
        shards, mesh=mesh, in_specs=placed, out_specs=P("rows", "cols"), check_vma=False
    )
```

```python
import jax
import jax.numpy as jnp
from jax import lax
from jax.experimental import pallas as pl
from jax.experimental.pallas import tpu as pltpu
from jax.sharding import PartitionSpec as P

NX, NY, NZ, NH, NC = 4, 4, 2, 4, 2
BF = jnp.bfloat16
F32 = jnp.float32


def row_id(x, y, z):
    return (x % NX) * (NY * NZ) + (y % NY) * NZ + (z % NZ)


def get_rows(value, dx=0, dy=0, dz=0):
    pairs = [
        (row_id(x + dx, y + dy, z + dz), row_id(x, y, z))
        for x in range(NX)
        for y in range(NY)
        for z in range(NZ)
    ]
    return lax.ppermute(value, "rows", pairs)


def get_x(value, k):
    return get_rows(value, dx=k)


def get_y(value, k):
    return get_rows(value, dy=k)


def get_z(value):
    return get_rows(value, dz=1)


def get_cols(value, dh=0, dc=0):
    pairs = [
        (((h + dh) % NH) * NC + (c + dc) % NC, h * NC + c) for h in range(NH) for c in range(NC)
    ]
    return lax.ppermute(value, "cols", pairs)


def dot(a, b, contract=((1,), (0,))):
    return lax.dot_general(a, b, (contract, ((), ())), preferred_element_type=F32)


def pick(natural, size):
    j = lax.broadcasted_iota(jnp.int32, (size, size), 1)
    k = lax.broadcasted_iota(jnp.int32, (size, size), 0)
    return jnp.where(k == natural(j), 1.0, 0.0).astype(BF)


def ring_gather(block, get):
    half = block.shape[0] // 2
    one = get(block, 1)
    three = get(block, 3)
    two_a = get(one[:half], 1)
    two_b = get(three[half:], 3)
    return jnp.concatenate([block, one, two_a, two_b, three], axis=0)


def direct_gather(block, get):
    return jnp.concatenate([block] + [get(block, k) for k in (1, 2, 3)], axis=0)


def direct_reduce(parts, get):
    sent = parts.astype(BF)
    total = parts[0]
    for k in (1, 2, 3):
        total = total + get(sent[(4 - k) % 4], k).astype(F32)
    return total


def local_call(kernel, outs, args, scratch=(), flops=0):
    specs = [pl.BlockSpec(memory_space=pltpu.VMEM)] * len(args)
    size = sum(a.size * a.dtype.itemsize for a in args)
    return pl.pallas_call(
        kernel,
        out_shape=outs,
        in_specs=specs,
        out_specs=pl.BlockSpec(memory_space=pltpu.VMEM),
        scratch_shapes=list(scratch),
        compiler_params=pltpu.CompilerParams(vmem_limit_bytes=24 * 1024 * 1024),
        cost_estimate=pl.CostEstimate(flops=flops, bytes_accessed=size, transcendentals=0),
    )(*args)


def blocks():
    for k in range(4):
        for hs in range(NH):
            for ys in range(2):
                for xs in range(NX):
                    for zs in range(NZ):
                        dest = row_id(xs, (k % 2) * 2 + ys, zs)
                        yield k, hs * 256 + ys * 128 + xs * 32, zs, dest, (k // 2) * 128 + hs * 32


def cross_kernel(c0, c1, c2, c3, out):
    chunks = (c0, c1, c2, c3)
    for k, row, zs, dest, place in blocks():
        out[dest, place : place + 32, :] = chunks[k][row : row + 32, zs * 128 : (zs + 1) * 128]


def fit_kernel(p0, p1, p2, p3, sol, treat, cot, u, table):
    @pl.when(pl.program_id(0) == 0)
    def _():
        for k, row, zs, dest, place in blocks():
            table[k, row : row + 32, zs * 128 : (zs + 1) * 128] = sol[dest, place : place + 32, :]

    fitted = jnp.dot(p0[...], table[0], preferred_element_type=F32)
    fitted = fitted + jnp.dot(p1[...], table[1], preferred_element_type=F32)
    fitted = fitted + jnp.dot(p2[...], table[2], preferred_element_type=F32)
    fitted = fitted + jnp.dot(p3[...], table[3], preferred_element_type=F32)
    u[:, 0:128] = (cot[...].astype(F32) - fitted[:, 128:256]).astype(BF)
    u[:, 128:256] = (treat[...].astype(F32) - fitted[:, 0:128]).astype(BF)


def fit_call(psis, sol, treat, cot):
    n = treat.shape[0]
    tile = 128
    rows = lambda width: pl.BlockSpec((tile, width), lambda i: (i, 0))
    return pl.pallas_call(
        fit_kernel,
        grid=(n // tile,),
        out_shape=jax.ShapeDtypeStruct((n, 256), BF),
        in_specs=[rows(1024)] * 4
        + [pl.BlockSpec((32, 256, 128), lambda i: (0, 0, 0)), rows(128), rows(128)],
        out_specs=rows(256),
        scratch_shapes=[pltpu.VMEM((4, 1024, 256), BF)],
        compiler_params=pltpu.CompilerParams(vmem_limit_bytes=14 * 1024 * 1024),
        cost_estimate=pl.CostEstimate(
            flops=2 * n * 4096 * 256, bytes_accessed=n * 9216 + 2**21, transcendentals=0
        ),
    )(*psis, sol, treat, cot)


def grad_kernel(*refs):
    parts, (got, slope, hidden_t, out, table, dpre) = refs[:16], refs[16:]
    for k in range(8):
        for xs in range(NX):
            for ys in range(NY):
                for zs in range(NZ):
                    row = (ys * NX + xs) * 32
                    table[k, row : row + 32, zs * 128 : (zs + 1) * 128] = got[
                        row_id(xs, ys, zs), k
                    ]
    half = parts[0].shape[0]
    tile = 128
    for side in range(2):

        @pl.loop(0, half // tile)
        def _(i):
            rows = pl.ds(pl.multiple_of(i * tile, tile), tile)
            total = None
            for k in range(8):
                left = parts[(k // 2) * 4 + (k % 2) * 2 + side][rows, :]
                term = lax.dot_general(
                    left, table[k], (((1,), (1,)), ((), ())), preferred_element_type=F32
                )
                total = term if total is None else total + term
            there = pl.ds(pl.multiple_of(side * half + i * tile, tile), tile)
            dpre[there, :] = (total * slope[there, :]).astype(BF)

    @pl.loop(0, hidden_t.shape[0] // 256)
    def _(i):
        rows = pl.ds(pl.multiple_of(i * 256, 256), 256)
        out[rows, :] = jnp.dot(
            hidden_t[rows, :], dpre[...], preferred_element_type=F32
        ).astype(BF)


def silu(v):
    return (0.5 * v) * (1.0 + jnp.tanh(0.5 * v))


def shards(hidden_in, w_out, inv_factor, treat_feat, section_cot):
    n_here = hidden_in.shape[0]
    row_total = n_here * lax.axis_size("rows")
    r = lax.axis_index("rows")
    c = lax.axis_index("cols")
    x, y, z = r // (NY * NZ), (r // NZ) % NY, r % NZ
    h, core = c // NC, c % NC

    def w_part(part):
        return jnp.concatenate(
            [
                lax.dynamic_slice(w_out, (0, (2 * hs + core) * 512 + part * 256), (32, 256))
                for hs in range(NH)
            ],
            axis=1,
        )

    w_half = jnp.stack([w_part(0), w_part(1)])
    w_pair = jnp.concatenate([w_half, get_z(w_half)], axis=1)
    w_pair, inv_factor = lax.optimization_barrier((w_pair, inv_factor))
    w_a = direct_gather(w_pair[0], get_x)
    w_b = direct_gather(w_pair[1], get_y)
    w_a, w_b, hidden_late = lax.optimization_barrier((w_a, w_b, hidden_in))
    w_a = ring_gather(w_a, get_y)
    w_b = ring_gather(w_b, get_x)

    def natural_a(j):
        ys, xs, zs, i = j // 256, (j // 64) % 4, (j // 32) % 2, j % 32
        return ((x + xs) % 4) * 256 + ((y + ys) % 4) * 64 + ((z + zs) % 2) * 32 + i

    def natural_b(j):
        xs, ys, zs, i = j // 256, (j // 64) % 4, (j // 32) % 2, j % 32
        return ((x + xs) % 4) * 256 + ((y + ys) % 4) * 64 + ((z + zs) % 2) * 32 + i

    h_a = dot(hidden_late, pick(natural_a, 1024)).astype(BF)
    h_b = dot(hidden_late, pick(natural_b, 1024)).astype(BF)

    l_half = lax.dynamic_slice_in_dim(inv_factor, core * 64, 64, 0).astype(BF)
    l_half = l_half.reshape(64, NH * NC, NY, 128)

    def l_cols(k):
        return lax.dynamic_index_in_dim(l_half, (y + 4 - k) % 4, 2, keepdims=False).reshape(64, 1024)

    l_parts = jnp.stack([l_cols(0)] + [get_y(l_cols(k), k) for k in (1, 2, 3)])
    l_parts = jnp.concatenate([l_parts, get_z(l_parts)], axis=1)
    l_block = jnp.concatenate([l_parts, get_cols(l_parts, dc=1)], axis=1).reshape(1024, 1024)

    def natural_l(j):
        xs, rc, hs, i = j // 256, (j // 128) % 2, (j // 32) % 4, j % 32
        return (hs * 2 + (core + rc) % 2) * 128 + ((x + xs) % 4) * 32 + i

    w_a, w_b, l_block = lax.optimization_barrier((w_a, w_b, l_block))
    psi_a = silu(dot(h_a, w_a)).astype(BF)
    psi_a_other = get_cols(psi_a, dc=1)
    psi_b = silu(dot(h_b, w_b)).astype(BF)
    psi_b_other = get_cols(psi_b, dc=1)
    psis = [psi_a, psi_b, psi_a_other, psi_b_other]

    targets = jnp.concatenate([treat_feat, section_cot], axis=1)
    cross = [dot(p, targets, ((0,), (0,))).astype(BF) for p in psis]
    cross = local_call(cross_kernel, jax.ShapeDtypeStruct((32, 256, 128), BF), cross)
    cross, l_block = lax.optimization_barrier((cross, l_block))
    cross = lax.all_to_all(cross, "rows", 0, 0, tiled=True)
    l_block = dot(l_block, pick(natural_l, 1024)).astype(BF)
    cross = jnp.sum(cross.astype(F32), axis=0).astype(BF)

    cross = direct_gather(cross, get_x)
    middle = dot(l_block, cross).reshape(4, 256, 128)
    middle = direct_reduce(middle, get_y).astype(BF)
    middle = direct_gather(middle, get_y)
    solved = dot(l_block, middle, ((0,), (0,))).reshape(4, 256, 128)
    solved = direct_reduce(solved, get_x).astype(BF)

    own = solved.reshape(2, NH, 32, 128)
    other = get_cols(own[1], dc=1)
    own = jnp.stack([own[0], other], axis=1)
    own = jnp.concatenate(
        [lax.dynamic_slice_in_dim(own, h, 1, 0)]
        + [get_cols(lax.dynamic_slice_in_dim(own, (h + 4 - k) % 4, 1, 0), dh=k) for k in (1, 2, 3)]
    ).reshape(8, 32, 128)

    sol = lax.all_to_all(jnp.broadcast_to(solved[None], (32, 256, 128)), "rows", 0, 0, tiled=True)
    u = fit_call(psis, sol, treat_feat, section_cot)
    u, own = lax.optimization_barrier((u, own))

    half = n_here // 2
    top, bottom = u[:half], u[half:]
    one_top = get_cols(top, dh=1)
    three_bottom = get_cols(bottom, dh=3)
    one_bottom = get_cols(bottom, dh=1)
    three_top = get_cols(top, dh=3)
    two_top = get_cols(one_top, dh=1)
    two_bottom = get_cols(three_bottom, dh=3)
    sol2 = lax.all_to_all(jnp.broadcast_to(own[None], (32, 8, 32, 128)), "rows", 0, 0, tiled=True)

    def other(value):
        return get_cols(value, dc=1)

    us = [top, bottom, one_top, one_bottom, two_top, two_bottom, three_top, three_bottom]
    u_parts = []
    for k in range(4):
        u_parts += us[2 * k : 2 * k + 2] + [other(v) for v in us[2 * k : 2 * k + 2]]

    pre = jnp.concatenate(
        [
            dot(h_a, lax.dynamic_slice_in_dim(w_a, h * 256, 256, 1)),
            dot(h_b, lax.dynamic_slice_in_dim(w_b, h * 256, 256, 1)),
        ],
        axis=1,
    )
    sig = jax.nn.sigmoid(pre)
    slope = sig * (1.0 + pre * (1.0 - sig))
    grad = local_call(
        grad_kernel,
        jax.ShapeDtypeStruct((1024, 512), BF),
        u_parts + [sol2, slope, hidden_late.T],
        scratch=[
            pltpu.VMEM((8, 512, 256), BF),
            pltpu.VMEM((n_here, 512), BF),
        ],
        flops=2 * n_here * 512 * 3072,
    ).reshape(32, 32, 512)
    grad = lax.all_to_all(grad, "rows", 0, 0, tiled=True)
    return jnp.sum(grad.astype(F32), axis=0) * (1.0 / jnp.sqrt(jnp.float32(row_total)))


def solution(mesh):
    placed = (
        P("rows", None),
        P("rows", None),
        P("rows", None),
        P("rows", "cols"),
        P("rows", "cols"),
    )
    return jax.shard_map(
        shards, mesh=mesh, in_specs=placed, out_specs=P("rows", "cols"), check_vma=False
    )
```

```python
import functools

import jax
import jax.numpy as jnp
from jax import lax
from jax.experimental import pallas as pl
from jax.experimental.pallas import tpu as pltpu
from jax.sharding import PartitionSpec as P

NX, NY, NZ, NH, NC = 4, 4, 2, 4, 2
BF = jnp.bfloat16
F32 = jnp.float32


def row_id(x, y, z):
    return (x % NX) * (NY * NZ) + (y % NY) * NZ + (z % NZ)


def get_rows(value, dx=0, dy=0, dz=0):
    pairs = [
        (row_id(x + dx, y + dy, z + dz), row_id(x, y, z))
        for x in range(NX)
        for y in range(NY)
        for z in range(NZ)
    ]
    return lax.ppermute(value, "rows", pairs)


def get_x(value, k):
    return get_rows(value, dx=k)


def get_y(value, k):
    return get_rows(value, dy=k)


def get_z(value):
    return get_rows(value, dz=1)


def get_cols(value, dh=0, dc=0):
    pairs = [
        (((h + dh) % NH) * NC + (c + dc) % NC, h * NC + c) for h in range(NH) for c in range(NC)
    ]
    return lax.ppermute(value, "cols", pairs)


def dot(a, b, contract=((1,), (0,))):
    return lax.dot_general(a, b, (contract, ((), ())), preferred_element_type=F32)


def pick(natural, size):
    j = lax.broadcasted_iota(jnp.int32, (size, size), 1)
    k = lax.broadcasted_iota(jnp.int32, (size, size), 0)
    return jnp.where(k == natural(j), 1.0, 0.0).astype(BF)


def ring_gather(block, get):
    half = block.shape[0] // 2
    one = get(block, 1)
    three = get(block, 3)
    two_a = get(one[:half], 1)
    two_b = get(three[half:], 3)
    return jnp.concatenate([block, one, two_a, two_b, three], axis=0)


def direct_gather(block, get):
    return jnp.concatenate([block] + [get(block, k) for k in (1, 2, 3)], axis=0)


def direct_reduce(parts, get):
    sent = parts.astype(BF)
    total = parts[0]
    for k in (1, 2, 3):
        total = total + get(sent[(4 - k) % 4], k).astype(F32)
    return total


def local_call(kernel, outs, args, scratch=(), flops=0, far=0):
    specs = [pl.BlockSpec(memory_space=pltpu.HBM)] * far
    specs += [pl.BlockSpec(memory_space=pltpu.VMEM)] * (len(args) - far)
    size = sum(a.size * a.dtype.itemsize for a in args)
    return pl.pallas_call(
        kernel,
        out_shape=outs,
        in_specs=specs,
        out_specs=jax.tree.map(lambda _: pl.BlockSpec(memory_space=pltpu.VMEM), outs),
        scratch_shapes=list(scratch),
        compiler_params=pltpu.CompilerParams(vmem_limit_bytes=28 * 1024 * 1024),
        cost_estimate=pl.CostEstimate(flops=flops, bytes_accessed=size, transcendentals=0),
    )(*args)


def blocks():
    for k in range(4):
        for hs in range(NH):
            for ys in range(2):
                for xs in range(NX):
                    for zs in range(NZ):
                        dest = row_id(xs, (k % 2) * 2 + ys, zs)
                        yield k, hs * 256 + ys * 128 + xs * 32, zs, dest, (k // 2) * 128 + hs * 32


def cross_kernel(c0, c1, c2, c3, out):
    chunks = (c0, c1, c2, c3)
    for k, row, zs, dest, place in blocks():
        out[dest, place : place + 32, :] = chunks[k][row : row + 32, zs * 128 : (zs + 1) * 128]


def fit_kernel(p0, p1, p2, p3, sol, treat, cot, u, psi, got, sems, table):
    copies = [pltpu.make_async_copy(sol, got, sems.at[4])]
    copies += [pltpu.make_async_copy(p, psi.at[k], sems.at[k]) for k, p in enumerate((p0, p1, p2, p3))]
    for copy in copies:
        copy.start()
    copies[0].wait()
    for k, row, zs, dest, place in blocks():
        table[k, row : row + 32, zs * 128 : (zs + 1) * 128] = got[dest, place : place + 32, :]
    for copy in copies[1:]:
        copy.wait()
    tile = 256

    @pl.loop(0, u.shape[0] // tile)
    def _(i):
        rows = pl.ds(pl.multiple_of(i * tile, tile), tile)
        fitted = jnp.dot(psi[0, rows, :], table[0], preferred_element_type=F32)
        for k in (1, 2, 3):
            fitted = fitted + jnp.dot(psi[k, rows, :], table[k], preferred_element_type=F32)
        u[rows, 0:128] = (cot[rows, :].astype(F32) - fitted[:, 128:256]).astype(BF)
        u[rows, 128:256] = (treat[rows, :].astype(F32) - fitted[:, 0:128]).astype(BF)


def grad_kernel(
    part, sol, sol_other, hidden_far, u, u_other, steep, own, one, two_top, two_bottom, three,
    got, hidden, sems, table, dpre,
):
    moves = [
        (sol.at[:, pl.ds(0, 128)], got.at[0]),
        (sol_other, got.at[1]),
        (hidden_far, hidden),
    ]
    copies = [pltpu.make_async_copy(a, b, sems.at[i]) for i, (a, b) in enumerate(moves)]
    for copy in copies:
        copy.start()
    copies[0].wait()
    copies[1].wait()
    for k, row, zs, dest, place in blocks():
        if k == part:
            for side in range(2):
                table[side, row : row + 32, zs * 128 : (zs + 1) * 128] = got[
                    side, dest, place : place + 32, :
                ]
    tile = 256

    @pl.loop(0, dpre.shape[0] // tile)
    def _(i):
        rows = pl.ds(pl.multiple_of(i * tile, tile), tile)
        for lo in range(0, 1024, 256):
            terms = [
                lax.dot_general(
                    left[rows, :],
                    table[side, lo : lo + 256, :],
                    (((1,), (1,)), ((), ())),
                    preferred_element_type=F32,
                )
                for side, left in enumerate((u, u_other))
            ]
            dpre[rows, lo : lo + 256] = (
                (terms[0] + terms[1]) * steep[rows, lo : lo + 256]
            ).astype(BF)

    copies[2].wait()
    start = 0
    for out in (own, one, two_top, two_bottom, three):
        for lo in range(0, 1024, 256):
            out[:, lo : lo + 256] = jnp.dot(
                hidden[start : start + out.shape[0], :],
                dpre[:, lo : lo + 256],
                preferred_element_type=F32,
            ).astype(BF)
        start += out.shape[0]


def ring_reduce(pieces, get):
    own, one, two_top, two_bottom, three = pieces
    half = two_top.shape[0]
    from_three = get(two_top, 3)
    from_one = get(two_bottom, 1)
    one = jnp.concatenate([(one[:half].astype(F32) + from_three.astype(F32)).astype(BF), one[half:]])
    three = jnp.concatenate([three[:half], (three[half:].astype(F32) + from_one.astype(F32)).astype(BF)])
    return own.astype(F32) + get(one, 3).astype(F32) + get(three, 1).astype(F32)


def slope(v):
    sig = 0.5 * (1.0 + jnp.tanh(0.5 * v))
    return sig * (1.0 + v * (1.0 - sig))


def silu(v):
    return (0.5 * v) * (1.0 + jnp.tanh(0.5 * v))


def shards(hidden_in, w_out, inv_factor, treat_feat, section_cot):
    n_here = hidden_in.shape[0]
    row_total = n_here * lax.axis_size("rows")
    r = lax.axis_index("rows")
    c = lax.axis_index("cols")
    x, y, z = r // (NY * NZ), (r // NZ) % NY, r % NZ
    h, core = c // NC, c % NC

    def w_part(part):
        return jnp.concatenate(
            [
                lax.dynamic_slice(w_out, (0, (2 * hs + core) * 512 + part * 256), (32, 256))
                for hs in range(NH)
            ],
            axis=1,
        )

    w_half = jnp.stack([w_part(0), w_part(1)])
    w_pair = jnp.concatenate([w_half, get_z(w_half)], axis=1)
    w_pair, inv_factor = lax.optimization_barrier((w_pair, inv_factor))
    w_a = direct_gather(w_pair[0], get_x)
    w_b = direct_gather(w_pair[1], get_y)
    w_a, w_b, hidden_late = lax.optimization_barrier((w_a, w_b, hidden_in))
    w_a = ring_gather(w_a, get_y)
    w_b = ring_gather(w_b, get_x)

    def natural_a(j):
        ys, xs, zs, i = j // 256, (j // 64) % 4, (j // 32) % 2, j % 32
        return ((x + xs) % 4) * 256 + ((y + ys) % 4) * 64 + ((z + zs) % 2) * 32 + i

    def natural_b(j):
        xs, ys, zs, i = j // 256, (j // 64) % 4, (j // 32) % 2, j % 32
        return ((x + xs) % 4) * 256 + ((y + ys) % 4) * 64 + ((z + zs) % 2) * 32 + i

    h_a = dot(pick(natural_a, 1024), hidden_late, ((0,), (1,))).astype(BF)
    h_b = dot(pick(natural_b, 1024), hidden_late, ((0,), (1,))).astype(BF)

    l_half = lax.dynamic_slice_in_dim(inv_factor, core * 64, 64, 0).astype(BF)
    l_half = jnp.concatenate([l_half, get_z(l_half)], axis=0)

    def natural_l(j):
        xs, rc, hs, i = j // 256, (j // 128) % 2, (j // 32) % 4, j % 32
        return (hs * 2 + (core + rc) % 2) * 128 + ((x + xs) % 4) * 32 + i

    w_a, w_b, l_half = lax.optimization_barrier((w_a, w_b, l_half))
    psi_a = silu(dot(h_a, w_a, ((0,), (0,)))).astype(BF)
    psi_a_other = get_cols(psi_a, dc=1)
    psi_b = silu(dot(h_b, w_b, ((0,), (0,)))).astype(BF)
    psi_b_other = get_cols(psi_b, dc=1)
    psis = [psi_a, psi_b, psi_a_other, psi_b_other]

    targets = jnp.concatenate([treat_feat, section_cot], axis=1)
    cross = [dot(p, targets, ((0,), (0,))).astype(BF) for p in psis]
    cross = local_call(cross_kernel, jax.ShapeDtypeStruct((32, 256, 128), BF), cross)
    cross, w_a, w_b, l_half = lax.optimization_barrier((cross, w_a, w_b, l_half))

    def l_cols(k):
        column = (y + 4 - k) % 4
        return jnp.concatenate(
            [
                lax.dynamic_slice(l_half, (0, (i * NY + column) * 128), (128, 128))
                for i in range(NH * NC)
            ],
            axis=1,
        )

    l_parts = jnp.stack([l_cols(0)] + [get_y(l_cols(k), k) for k in (1, 2, 3)])

    slope_a = slope(dot(h_a, w_a, ((0,), (0,))))
    slope_b = slope(dot(h_b, w_b, ((0,), (0,))))
    cross = lax.all_to_all(cross, "rows", 0, 0, tiled=True)
    l_block = jnp.concatenate([l_parts, get_cols(l_parts, dc=1)], axis=1).reshape(1024, 1024)
    l_block = dot(l_block, pick(natural_l, 1024)).astype(BF)
    cross, l_block, slope_a, slope_b = lax.optimization_barrier((cross, l_block, slope_a, slope_b))
    cross = jnp.sum(cross.astype(F32), axis=0).astype(BF)

    cross = direct_gather(cross, get_x)
    middle = dot(l_block, cross).reshape(4, 256, 128)
    middle = direct_reduce(middle, get_y).astype(BF)
    middle = direct_gather(middle, get_y)
    solved = dot(l_block, middle, ((0,), (0,))).reshape(4, 256, 128)
    solved = direct_reduce(solved, get_x).astype(BF)

    sol = lax.all_to_all(jnp.broadcast_to(solved[None], (32, 256, 128)), "rows", 0, 0, tiled=True)
    sol_other = get_cols(sol[:, 128:], dc=1)
    n_width = 2 * treat_feat.shape[1]
    u = local_call(
        fit_kernel,
        jax.ShapeDtypeStruct((n_here, n_width), BF),
        psis + [sol, treat_feat, section_cot],
        scratch=[
            pltpu.VMEM((4, n_here, 1024), BF),
            pltpu.VMEM((32, 256, 128), BF),
            pltpu.SemaphoreType.DMA((5,)),
            pltpu.VMEM((4, 1024, n_width), BF),
        ],
        flops=2 * n_here * 4096 * n_width,
        far=5,
    )
    u_other = get_cols(u, dc=1)

    def grad_part(part, hidden, steep):
        return local_call(
            functools.partial(grad_kernel, part),
            [jax.ShapeDtypeStruct((n, 1024), BF) for n in (256, 256, 128, 128, 256)],
            [sol, sol_other, hidden, u, u_other, steep],
            scratch=[
                pltpu.VMEM((2, 32, 128, 128), BF),
                pltpu.VMEM((1024, n_here), BF),
                pltpu.SemaphoreType.DMA((3,)),
                pltpu.VMEM((2, 1024, n_width), BF),
                pltpu.VMEM((n_here, 1024), BF),
            ],
            flops=2 * n_here * 1024 * 1536,
            far=3,
        )

    grad_a = ring_reduce(grad_part(0, h_b, slope_a), get_x).reshape(4, 64, 1024)
    grad_b = ring_reduce(grad_part(1, h_a, slope_b), get_y).reshape(4, 64, 1024)
    grad_a = direct_reduce(grad_a, get_y)
    grad_b = direct_reduce(grad_b, get_x)
    kept = jnp.stack([grad_a[:32], grad_b[:32]])
    sent = jnp.stack([grad_a[32:], grad_b[32:]]).astype(BF)
    grad = (kept + get_z(sent).astype(F32)).reshape(2, 32, NH, 256)

    def for_h(k):
        return lax.dynamic_index_in_dim(grad, (h + 4 - k) % 4, 2, keepdims=False)

    total = for_h(0)
    for k in (1, 2, 3):
        total = total + get_cols(for_h(k).astype(BF), dh=k).astype(F32)
    total = jnp.concatenate([total[0], total[1]], axis=1)
    return total * (1.0 / jnp.sqrt(jnp.float32(row_total)))


def solution(mesh):
    placed = (
        P("rows", None),
        P("rows", None),
        P("rows", None),
        P("rows", "cols"),
        P("rows", "cols"),
    )
    return jax.shard_map(
        shards, mesh=mesh, in_specs=placed, out_specs=P("rows", "cols"), check_vma=False
    )
```

```python
import functools

import jax
import jax.numpy as jnp
from jax import lax
from jax.experimental import pallas as pl
from jax.experimental.pallas import tpu as pltpu
from jax.sharding import PartitionSpec as P

NX, NY, NZ, NH, NC = 4, 4, 2, 4, 2
BF = jnp.bfloat16
F32 = jnp.float32


def row_id(x, y, z):
    return (x % NX) * (NY * NZ) + (y % NY) * NZ + (z % NZ)


def get_rows(value, dx=0, dy=0, dz=0):
    pairs = [
        (row_id(x + dx, y + dy, z + dz), row_id(x, y, z))
        for x in range(NX)
        for y in range(NY)
        for z in range(NZ)
    ]
    return lax.ppermute(value, "rows", pairs)


def get_x(value, k):
    return get_rows(value, dx=k)


def get_y(value, k):
    return get_rows(value, dy=k)


def get_z(value):
    return get_rows(value, dz=1)


def get_cols(value, dh=0, dc=0):
    pairs = [
        (((h + dh) % NH) * NC + (c + dc) % NC, h * NC + c) for h in range(NH) for c in range(NC)
    ]
    return lax.ppermute(value, "cols", pairs)


def dot(a, b, contract=((1,), (0,))):
    return lax.dot_general(a, b, (contract, ((), ())), preferred_element_type=F32)


def pick(natural, size):
    j = lax.broadcasted_iota(jnp.int32, (size, size), 1)
    k = lax.broadcasted_iota(jnp.int32, (size, size), 0)
    return jnp.where(k == natural(j), 1.0, 0.0).astype(BF)


def ring_gather(block, get):
    half = block.shape[0] // 2
    one = get(block, 1)
    three = get(block, 3)
    two_a = get(one[:half], 1)
    two_b = get(three[half:], 3)
    return jnp.concatenate([block, one, two_a, two_b, three], axis=0)


def direct_gather(block, get):
    return jnp.concatenate([block] + [get(block, k) for k in (1, 2, 3)], axis=0)


def direct_reduce(parts, get):
    sent = parts.astype(BF)
    total = parts[0]
    for k in (1, 2, 3):
        total = total + get(sent[(4 - k) % 4], k).astype(F32)
    return total


def local_call(kernel, outs, args, scratch=(), flops=0, far=0):
    specs = [pl.BlockSpec(memory_space=pltpu.HBM)] * far
    specs += [pl.BlockSpec(memory_space=pltpu.VMEM)] * (len(args) - far)
    size = sum(a.size * a.dtype.itemsize for a in args)
    return pl.pallas_call(
        kernel,
        out_shape=outs,
        in_specs=specs,
        out_specs=jax.tree.map(lambda _: pl.BlockSpec(memory_space=pltpu.VMEM), outs),
        scratch_shapes=list(scratch),
        compiler_params=pltpu.CompilerParams(vmem_limit_bytes=(56 if far else 16) * 1024 * 1024),
        cost_estimate=pl.CostEstimate(flops=flops, bytes_accessed=size, transcendentals=0),
    )(*args)


def blocks():
    for k in range(4):
        for hs in range(NH):
            for ys in range(2):
                for xs in range(NX):
                    for zs in range(NZ):
                        dest = row_id(xs, (k % 2) * 2 + ys, zs)
                        yield k, hs * 256 + ys * 128 + xs * 32, zs, dest, (k // 2) * 128 + hs * 32


def cross_kernel(c0, c1, c2, c3, out):
    chunks = (c0, c1, c2, c3)
    for k, row, zs, dest, place in blocks():
        out[dest, place : place + 32, :] = chunks[k][row : row + 32, zs * 128 : (zs + 1) * 128]


def fit_kernel(p0, p1, p2, p3, sol, treat, cot, u, psi, got, sems, table):
    copies = [pltpu.make_async_copy(sol, got, sems.at[4])]
    copies += [pltpu.make_async_copy(p, psi.at[k], sems.at[k]) for k, p in enumerate((p0, p1, p2, p3))]
    for copy in copies:
        copy.start()
    copies[0].wait()
    for k, row, zs, dest, place in blocks():
        table[k, row : row + 32, zs * 128 : (zs + 1) * 128] = got[dest, place : place + 32, :]
    for copy in copies[1:]:
        copy.wait()
    tile = 256

    @pl.loop(0, u.shape[0] // tile)
    def _(i):
        rows = pl.ds(pl.multiple_of(i * tile, tile), tile)
        fitted = jnp.dot(psi[0, rows, :], table[0], preferred_element_type=F32)
        for k in (1, 2, 3):
            fitted = fitted + jnp.dot(psi[k, rows, :], table[k], preferred_element_type=F32)
        u[rows, 0:128] = (cot[rows, :].astype(F32) - fitted[:, 128:256]).astype(BF)
        u[rows, 128:256] = (treat[rows, :].astype(F32) - fitted[:, 0:128]).astype(BF)


def grad_kernel(
    part, sol, sol_other, hidden_far, u, u_other, steep, own, one, two_top, two_bottom, three,
    got, hidden, sems, table, dpre,
):
    moves = [
        (sol.at[:, pl.ds(0, 128)], got.at[0]),
        (sol_other, got.at[1]),
        (hidden_far, hidden),
    ]
    copies = [pltpu.make_async_copy(a, b, sems.at[i]) for i, (a, b) in enumerate(moves)]
    for copy in copies:
        copy.start()
    copies[0].wait()
    copies[1].wait()
    for k, row, zs, dest, place in blocks():
        if k == part:
            for side in range(2):
                table[side, row : row + 32, zs * 128 : (zs + 1) * 128] = got[
                    side, dest, place : place + 32, :
                ]
    tile = 256

    @pl.loop(0, dpre.shape[0] // tile)
    def _(i):
        rows = pl.ds(pl.multiple_of(i * tile, tile), tile)
        for lo in range(0, 1024, 256):
            terms = [
                lax.dot_general(
                    left[rows, :],
                    table[side, lo : lo + 256, :],
                    (((1,), (1,)), ((), ())),
                    preferred_element_type=F32,
                )
                for side, left in enumerate((u, u_other))
            ]
            dpre[rows, lo : lo + 256] = (
                (terms[0] + terms[1]) * steep[rows, lo : lo + 256]
            ).astype(BF)

    copies[2].wait()
    start = 0
    for out in (own, one, two_top, two_bottom, three):
        for lo in range(0, 1024, 256):
            out[:, lo : lo + 256] = jnp.dot(
                hidden[start : start + out.shape[0], :],
                dpre[:, lo : lo + 256],
                preferred_element_type=F32,
            ).astype(BF)
        start += out.shape[0]


def ring_reduce(pieces, get):
    own, one, two_top, two_bottom, three = pieces
    half = two_top.shape[0]
    from_three = get(two_top, 3)
    from_one = get(two_bottom, 1)
    one = jnp.concatenate([(one[:half].astype(F32) + from_three.astype(F32)).astype(BF), one[half:]])
    three = jnp.concatenate([three[:half], (three[half:].astype(F32) + from_one.astype(F32)).astype(BF)])
    return own.astype(F32) + get(one, 3).astype(F32) + get(three, 1).astype(F32)


def slope(v):
    sig = 0.5 * (1.0 + jnp.tanh(0.5 * v))
    return sig * (1.0 + v * (1.0 - sig))


def silu(v):
    return (0.5 * v) * (1.0 + jnp.tanh(0.5 * v))


def shards(hidden_in, w_out, inv_factor, treat_feat, section_cot):
    n_here = hidden_in.shape[0]
    row_total = n_here * lax.axis_size("rows")
    r = lax.axis_index("rows")
    c = lax.axis_index("cols")
    x, y, z = r // (NY * NZ), (r // NZ) % NY, r % NZ
    h, core = c // NC, c % NC

    def w_part(part):
        return jnp.concatenate(
            [
                lax.dynamic_slice(w_out, (0, (2 * hs + core) * 512 + part * 256), (32, 256))
                for hs in range(NH)
            ],
            axis=1,
        )

    w_half = jnp.stack([w_part(0), w_part(1)])
    w_pair = jnp.concatenate([w_half, get_z(w_half)], axis=1)
    w_pair, inv_factor = lax.optimization_barrier((w_pair, inv_factor))
    w_a = direct_gather(w_pair[0], get_x)
    w_b = direct_gather(w_pair[1], get_y)
    w_a, w_b, hidden_late = lax.optimization_barrier((w_a, w_b, hidden_in))
    w_a = ring_gather(w_a, get_y)
    w_b = ring_gather(w_b, get_x)

    def natural_a(j):
        ys, xs, zs, i = j // 256, (j // 64) % 4, (j // 32) % 2, j % 32
        return ((x + xs) % 4) * 256 + ((y + ys) % 4) * 64 + ((z + zs) % 2) * 32 + i

    def natural_b(j):
        xs, ys, zs, i = j // 256, (j // 64) % 4, (j // 32) % 2, j % 32
        return ((x + xs) % 4) * 256 + ((y + ys) % 4) * 64 + ((z + zs) % 2) * 32 + i

    h_a = dot(pick(natural_a, 1024), hidden_late, ((0,), (1,))).astype(BF)
    h_b = dot(pick(natural_b, 1024), hidden_late, ((0,), (1,))).astype(BF)

    l_half = lax.dynamic_slice_in_dim(inv_factor, core * 64, 64, 0).astype(BF)
    l_half = jnp.concatenate([l_half, get_z(l_half)], axis=0)

    def natural_l(j):
        xs, rc, hs, i = j // 256, (j // 128) % 2, (j // 32) % 4, j % 32
        return (hs * 2 + (core + rc) % 2) * 128 + ((x + xs) % 4) * 32 + i

    def l_cols(k):
        column = (y + 4 - k) % 4
        return jnp.concatenate(
            [
                lax.dynamic_slice(l_half, (0, (i * NY + column) * 128), (128, 128))
                for i in range(NH * NC)
            ],
            axis=1,
        )

    l_parts = [l_cols(k) for k in range(4)]
    w_a, w_b, l_parts = lax.optimization_barrier((w_a, w_b, l_parts))
    psi_a = silu(dot(h_a, w_a, ((0,), (0,)))).astype(BF)
    psi_a_other = get_cols(psi_a, dc=1)
    psi_a, l_parts = lax.optimization_barrier((psi_a, l_parts))
    l_parts = [l_parts[0]] + [get_y(l_parts[k], k) for k in (1, 2, 3)]
    psi_b = silu(dot(h_b, w_b, ((0,), (0,)))).astype(BF)
    psi_b_other = get_cols(psi_b, dc=1)
    psis = [psi_a, psi_b, psi_a_other, psi_b_other]

    targets = jnp.concatenate([treat_feat, section_cot], axis=1)
    cross = [dot(p, targets, ((0,), (0,))).astype(BF) for p in psis]
    cross = local_call(cross_kernel, jax.ShapeDtypeStruct((32, 256, 128), BF), cross)
    cross, l_parts = lax.optimization_barrier((cross, l_parts))
    l_parts = jnp.stack(l_parts)
    cross = lax.all_to_all(cross, "rows", 0, 0, tiled=True)
    l_block = jnp.concatenate([l_parts, get_cols(l_parts, dc=1)], axis=1).reshape(1024, 1024)
    l_block = dot(l_block, pick(natural_l, 1024)).astype(BF)
    cross, l_block = lax.optimization_barrier((cross, l_block))
    cross = jnp.sum(cross.astype(F32), axis=0).astype(BF)

    cross = direct_gather(cross, get_x)
    middle = dot(l_block, cross).reshape(4, 256, 128)
    middle = direct_reduce(middle, get_y).astype(BF)
    middle = direct_gather(middle, get_y)
    solved = dot(l_block, middle, ((0,), (0,))).reshape(4, 256, 128)
    solved = direct_reduce(solved, get_x).astype(BF)

    solved, w_a, w_b = lax.optimization_barrier((solved, w_a, w_b))
    slope_a = slope(dot(h_a, w_a, ((0,), (0,))))
    slope_b = slope(dot(h_b, w_b, ((0,), (0,))))
    sol = lax.all_to_all(jnp.broadcast_to(solved[None], (32, 256, 128)), "rows", 0, 0, tiled=True)
    sol, slope_a, slope_b = lax.optimization_barrier((sol, slope_a, slope_b))
    sol_other = get_cols(sol[:, 128:], dc=1)
    n_width = 2 * treat_feat.shape[1]
    u = local_call(
        fit_kernel,
        jax.ShapeDtypeStruct((n_here, n_width), BF),
        psis + [sol, treat_feat, section_cot],
        scratch=[
            pltpu.VMEM((4, n_here, 1024), BF),
            pltpu.VMEM((32, 256, 128), BF),
            pltpu.SemaphoreType.DMA((5,)),
            pltpu.VMEM((4, 1024, n_width), BF),
        ],
        flops=2 * n_here * 4096 * n_width,
        far=5,
    )
    u_other = get_cols(u, dc=1)

    def grad_part(part, hidden, steep):
        return local_call(
            functools.partial(grad_kernel, part),
            [jax.ShapeDtypeStruct((n, 1024), BF) for n in (256, 256, 128, 128, 256)],
            [sol, sol_other, hidden, u, u_other, steep],
            scratch=[
                pltpu.VMEM((2, 32, 128, 128), BF),
                pltpu.VMEM((1024, n_here), BF),
                pltpu.SemaphoreType.DMA((3,)),
                pltpu.VMEM((2, 1024, n_width), BF),
                pltpu.VMEM((n_here, 1024), BF),
            ],
            flops=2 * n_here * 1024 * 1536,
            far=3,
        )

    grad_a = ring_reduce(grad_part(0, h_b, slope_a), get_x).reshape(4, 64, 1024)
    grad_b = ring_reduce(grad_part(1, h_a, slope_b), get_y).reshape(4, 64, 1024)
    grad_a = direct_reduce(grad_a, get_y)
    grad_b = direct_reduce(grad_b, get_x)
    kept = jnp.stack([grad_a[:32], grad_b[:32]])
    sent = jnp.stack([grad_a[32:], grad_b[32:]]).astype(BF)
    grad = (kept + get_z(sent).astype(F32)).reshape(2, 32, NH, 256)

    def for_h(k):
        return lax.dynamic_index_in_dim(grad, (h + 4 - k) % 4, 2, keepdims=False)

    total = for_h(0)
    for k in (1, 2, 3):
        total = total + get_cols(for_h(k).astype(BF), dh=k).astype(F32)
    total = jnp.concatenate([total[0], total[1]], axis=1)
    return total * (1.0 / jnp.sqrt(jnp.float32(row_total)))


def solution(mesh):
    placed = (
        P("rows", None),
        P("rows", None),
        P("rows", None),
        P("rows", "cols"),
        P("rows", "cols"),
    )
    return jax.shard_map(
        shards, mesh=mesh, in_specs=placed, out_specs=P("rows", "cols"), check_vma=False
    )
```

```python
import functools

import jax
import jax.numpy as jnp
from jax import lax
from jax.experimental import pallas as pl
from jax.experimental.pallas import tpu as pltpu
from jax.sharding import PartitionSpec as P

NX, NY, NZ, NH, NC = 4, 4, 2, 4, 2
BF = jnp.bfloat16
F32 = jnp.float32


def row_id(x, y, z):
    return (x % NX) * (NY * NZ) + (y % NY) * NZ + (z % NZ)


def get_rows(value, dx=0, dy=0, dz=0):
    pairs = [
        (row_id(x + dx, y + dy, z + dz), row_id(x, y, z))
        for x in range(NX)
        for y in range(NY)
        for z in range(NZ)
    ]
    return lax.ppermute(value, "rows", pairs)


def get_x(value, k):
    return get_rows(value, dx=k)


def get_y(value, k):
    return get_rows(value, dy=k)


def get_z(value):
    return get_rows(value, dz=1)


def get_cols(value, dh=0, dc=0):
    pairs = [
        (((h + dh) % NH) * NC + (c + dc) % NC, h * NC + c) for h in range(NH) for c in range(NC)
    ]
    return lax.ppermute(value, "cols", pairs)


def dot(a, b, contract=((1,), (0,))):
    return lax.dot_general(a, b, (contract, ((), ())), preferred_element_type=F32)


def pick(natural, size):
    j = lax.broadcasted_iota(jnp.int32, (size, size), 1)
    k = lax.broadcasted_iota(jnp.int32, (size, size), 0)
    return jnp.where(k == natural(j), 1.0, 0.0).astype(BF)


def ring_gather(block, get):
    half = block.shape[0] // 2
    one = get(block, 1)
    three = get(block, 3)
    two_a = get(one[:half], 1)
    two_b = get(three[half:], 3)
    return jnp.concatenate([block, one, two_a, two_b, three], axis=0)


def direct_gather(block, get):
    return jnp.concatenate([block] + [get(block, k) for k in (1, 2, 3)], axis=0)


def direct_reduce(parts, get):
    sent = parts.astype(BF)
    total = parts[0]
    for k in (1, 2, 3):
        total = total + get(sent[(4 - k) % 4], k).astype(F32)
    return total


def local_call(kernel, outs, args, scratch=(), flops=0, far=0, far_out=False):
    specs = [pl.BlockSpec(memory_space=pltpu.HBM)] * far
    specs += [pl.BlockSpec(memory_space=pltpu.VMEM)] * (len(args) - far)
    size = sum(a.size * a.dtype.itemsize for a in args)
    space = pltpu.HBM if far_out else pltpu.VMEM
    return pl.pallas_call(
        kernel,
        out_shape=outs,
        in_specs=specs,
        out_specs=jax.tree.map(lambda _: pl.BlockSpec(memory_space=space), outs),
        scratch_shapes=list(scratch),
        compiler_params=pltpu.CompilerParams(vmem_limit_bytes=(56 if far else 16) * 1024 * 1024),
        cost_estimate=pl.CostEstimate(flops=flops, bytes_accessed=size, transcendentals=0),
    )(*args)


def blocks():
    for k in range(4):
        for hs in range(NH):
            for ys in range(2):
                for xs in range(NX):
                    for zs in range(NZ):
                        dest = row_id(xs, (k % 2) * 2 + ys, zs)
                        yield k, hs * 256 + ys * 128 + xs * 32, zs, dest, (k // 2) * 128 + hs * 32


def cross_kernel(c0, c1, c2, c3, out):
    chunks = (c0, c1, c2, c3)
    for k, row, zs, dest, place in blocks():
        out[dest, place : place + 32, :] = chunks[k][row : row + 32, zs * 128 : (zs + 1) * 128]


def fit_kernel(p0, p1, p2, p3, sol, treat, cot, u, psi, got, sems, table, fitted):
    first = pltpu.make_async_copy(sol, got, sems.at[4])
    first.start()
    copies = [pltpu.make_async_copy(p, psi.at[k], sems.at[k]) for k, p in enumerate((p0, p1, p2, p3))]
    for copy in copies:
        copy.start()
    first.wait()
    tile = 256
    for k in range(4):
        for kk, row, zs, dest, place in blocks():
            if kk == k:
                table[k, row : row + 32, zs * 128 : (zs + 1) * 128] = got[
                    dest, place : place + 32, :
                ]
        copies[k].wait()

        @pl.loop(0, u.shape[0] // tile)
        def _(i):
            rows = pl.ds(pl.multiple_of(i * tile, tile), tile)
            part = jnp.dot(psi[k, rows, :], table[k], preferred_element_type=F32)
            if k == 0:
                fitted[rows, :] = part
            elif k < 3:
                fitted[rows, :] += part
            else:
                part = fitted[rows, :] + part
                u[rows, 0:128] = (cot[rows, :].astype(F32) - part[:, 128:256]).astype(BF)
                u[rows, 128:256] = (treat[rows, :].astype(F32) - part[:, 0:128]).astype(BF)


def grad_kernel(
    part, sol, sol_other, u_far, other_far, steep_far, hidden_far,
    own, one, two_top, two_bottom, three,
    got, left, steep, hidden, result, sems, out_sems, table, dpre,
):
    moves = [
        (sol.at[:, pl.ds(0, 128)], got.at[0]),
        (sol_other, got.at[1]),
        (u_far, left.at[0]),
        (other_far, left.at[1]),
        (steep_far, steep),
        (hidden_far, hidden),
    ]
    copies = [pltpu.make_async_copy(a, b, sems.at[i]) for i, (a, b) in enumerate(moves)]
    for copy in copies:
        copy.start()
    for side in range(2):
        copies[side].wait()
        for k, row, zs, dest, place in blocks():
            if k == part:
                table[side, row : row + 32, zs * 128 : (zs + 1) * 128] = got[
                    side, dest, place : place + 32, :
                ]
    for copy in copies[2:5]:
        copy.wait()
    tile = 256

    @pl.loop(0, dpre.shape[0] // tile)
    def _(i):
        rows = pl.ds(pl.multiple_of(i * tile, tile), tile)
        for lo in range(0, 1024, 256):
            terms = [
                lax.dot_general(
                    left[side, rows, :],
                    table[side, lo : lo + 256, :],
                    (((1,), (1,)), ((), ())),
                    preferred_element_type=F32,
                )
                for side in range(2)
            ]
            dpre[rows, lo : lo + 256] = (
                (terms[0] + terms[1]) * steep[rows, lo : lo + 256]
            ).astype(BF)

    copies[5].wait()
    sent = []
    for i, out in enumerate((two_top, two_bottom, one, three, own)):
        start = (512, 640, 256, 768, 0)[i]
        n = out.shape[0]
        for lo in range(0, 1024, 256):
            result[start : start + n, lo : lo + 256] = jnp.dot(
                hidden[start : start + n, :],
                dpre[:, lo : lo + 256],
                preferred_element_type=F32,
            ).astype(BF)
        copy = pltpu.make_async_copy(result.at[pl.ds(start, n)], out, out_sems.at[i])
        copy.start()
        sent.append(copy)
    for copy in sent:
        copy.wait()


def ring_reduce(pieces, get):
    own, one, two_top, two_bottom, three = pieces
    half = two_top.shape[0]
    from_three = get(two_top, 3)
    from_one = get(two_bottom, 1)
    one = jnp.concatenate([(one[:half].astype(F32) + from_three.astype(F32)).astype(BF), one[half:]])
    three = jnp.concatenate([three[:half], (three[half:].astype(F32) + from_one.astype(F32)).astype(BF)])
    return own.astype(F32) + get(one, 3).astype(F32) + get(three, 1).astype(F32)


def slope(v):
    sig = 0.5 * (1.0 + jnp.tanh(0.5 * v))
    return sig * (1.0 + v * (1.0 - sig))


def silu(v):
    return (0.5 * v) * (1.0 + jnp.tanh(0.5 * v))


def shards(hidden_in, w_out, inv_factor, treat_feat, section_cot):
    n_here = hidden_in.shape[0]
    row_total = n_here * lax.axis_size("rows")
    r = lax.axis_index("rows")
    c = lax.axis_index("cols")
    x, y, z = r // (NY * NZ), (r // NZ) % NY, r % NZ
    h, core = c // NC, c % NC

    def w_part(part):
        return jnp.concatenate(
            [
                lax.dynamic_slice(w_out, (0, (2 * hs + core) * 512 + part * 256), (32, 256))
                for hs in range(NH)
            ],
            axis=1,
        )

    w_half = jnp.stack([w_part(0), w_part(1)])
    w_pair = jnp.concatenate([w_half, get_z(w_half)], axis=1)
    w_pair, inv_factor = lax.optimization_barrier((w_pair, inv_factor))
    w_a = direct_gather(w_pair[0], get_x)
    w_b = direct_gather(w_pair[1], get_y)
    w_a, w_b, hidden_late = lax.optimization_barrier((w_a, w_b, hidden_in))
    w_a = ring_gather(w_a, get_y)
    w_b = ring_gather(w_b, get_x)

    def natural_a(j):
        ys, xs, zs, i = j // 256, (j // 64) % 4, (j // 32) % 2, j % 32
        return ((x + xs) % 4) * 256 + ((y + ys) % 4) * 64 + ((z + zs) % 2) * 32 + i

    def natural_b(j):
        xs, ys, zs, i = j // 256, (j // 64) % 4, (j // 32) % 2, j % 32
        return ((x + xs) % 4) * 256 + ((y + ys) % 4) * 64 + ((z + zs) % 2) * 32 + i

    h_a = dot(pick(natural_a, 1024), hidden_late, ((0,), (1,))).astype(BF)
    h_b = dot(pick(natural_b, 1024), hidden_late, ((0,), (1,))).astype(BF)

    l_half = lax.dynamic_slice_in_dim(inv_factor, core * 64, 64, 0).astype(BF)
    l_half = jnp.concatenate([l_half, get_z(l_half)], axis=0)

    def natural_l(j):
        xs, rc, hs, i = j // 256, (j // 128) % 2, (j // 32) % 4, j % 32
        return (hs * 2 + (core + rc) % 2) * 128 + ((x + xs) % 4) * 32 + i

    def l_cols(k):
        column = (y + 4 - k) % 4
        return jnp.concatenate(
            [
                lax.dynamic_slice(l_half, (0, (i * NY + column) * 128), (128, 128))
                for i in range(NH * NC)
            ],
            axis=1,
        )

    l_parts = [l_cols(k) for k in range(4)]
    l_parts = [l_parts[0]] + [get_y(l_parts[k], k) for k in (1, 2, 3)]
    w_a, w_b, l_parts = lax.optimization_barrier((w_a, w_b, l_parts))
    psi_a = silu(dot(h_a, w_a, ((0,), (0,)))).astype(BF)
    psi_a_other = get_cols(psi_a, dc=1)
    psi_b = silu(dot(h_b, w_b, ((0,), (0,)))).astype(BF)
    psi_b_other = get_cols(psi_b, dc=1)
    psis = [psi_a, psi_b, psi_a_other, psi_b_other]

    targets = jnp.concatenate([treat_feat, section_cot], axis=1)
    cross = [dot(p, targets, ((0,), (0,))).astype(BF) for p in psis]
    cross = local_call(cross_kernel, jax.ShapeDtypeStruct((32, 256, 128), BF), cross)
    cross, l_parts = lax.optimization_barrier((cross, l_parts))
    l_parts = jnp.stack(l_parts)
    cross = lax.all_to_all(cross, "rows", 0, 0, tiled=True)
    l_block = jnp.concatenate([l_parts, get_cols(l_parts, dc=1)], axis=1).reshape(1024, 1024)
    l_block = dot(l_block, pick(natural_l, 1024)).astype(BF)
    cross, l_block = lax.optimization_barrier((cross, l_block))
    cross = jnp.sum(cross.astype(F32), axis=0).astype(BF)

    cross = direct_gather(cross, get_x)
    middle = dot(l_block, cross).reshape(4, 256, 128)
    middle = direct_reduce(middle, get_y).astype(BF)
    middle = direct_gather(middle, get_y)
    solved = dot(l_block, middle, ((0,), (0,))).reshape(4, 256, 128)
    solved = direct_reduce(solved, get_x).astype(BF)

    solved, w_a, w_b = lax.optimization_barrier((solved, w_a, w_b))
    slope_a = slope(dot(h_a, w_a, ((0,), (0,))))
    slope_b = slope(dot(h_b, w_b, ((0,), (0,))))
    sol = lax.all_to_all(jnp.broadcast_to(solved[None], (32, 256, 128)), "rows", 0, 0, tiled=True)
    sol, slope_a, slope_b = lax.optimization_barrier((sol, slope_a, slope_b))
    sol_other = get_cols(sol[:, 128:], dc=1)
    n_width = 2 * treat_feat.shape[1]
    u = local_call(
        fit_kernel,
        jax.ShapeDtypeStruct((n_here, n_width), BF),
        psis + [sol, treat_feat, section_cot],
        scratch=[
            pltpu.VMEM((4, n_here, 1024), BF),
            pltpu.VMEM((32, 256, 128), BF),
            pltpu.SemaphoreType.DMA((5,)),
            pltpu.VMEM((4, 1024, n_width), BF),
            pltpu.VMEM((n_here, n_width), F32),
        ],
        flops=2 * n_here * 4096 * n_width,
        far=5,
    )
    u_other = get_cols(u, dc=1)

    def grad_part(part, hidden, steep):
        return local_call(
            functools.partial(grad_kernel, part),
            [jax.ShapeDtypeStruct((n, 1024), BF) for n in (256, 256, 128, 128, 256)],
            [sol, sol_other, u, u_other, steep, hidden],
            scratch=[
                pltpu.VMEM((2, 32, 128, 128), BF),
                pltpu.VMEM((2, n_here, n_width), BF),
                pltpu.VMEM((n_here, 1024), F32),
                pltpu.VMEM((1024, n_here), BF),
                pltpu.VMEM((1024, 1024), BF),
                pltpu.SemaphoreType.DMA((6,)),
                pltpu.SemaphoreType.DMA((5,)),
                pltpu.VMEM((2, 1024, n_width), BF),
                pltpu.VMEM((n_here, 1024), BF),
            ],
            flops=2 * n_here * 1024 * 1536,
            far=6,
            far_out=True,
        )

    grad_a = ring_reduce(grad_part(0, h_b, slope_a), get_x).reshape(4, 64, 1024)
    grad_b = ring_reduce(grad_part(1, h_a, slope_b), get_y).reshape(4, 64, 1024)
    grad_a = direct_reduce(grad_a, get_y)
    grad_b = direct_reduce(grad_b, get_x)
    kept = jnp.stack([grad_a[:32], grad_b[:32]])
    sent = jnp.stack([grad_a[32:], grad_b[32:]]).astype(BF)
    grad = (kept + get_z(sent).astype(F32)).reshape(2, 32, NH, 256)

    def for_h(k):
        return lax.dynamic_index_in_dim(grad, (h + 4 - k) % 4, 2, keepdims=False)

    total = for_h(0)
    for k in (1, 2, 3):
        total = total + get_cols(for_h(k).astype(BF), dh=k).astype(F32)
    total = jnp.concatenate([total[0], total[1]], axis=1)
    return total * (1.0 / jnp.sqrt(jnp.float32(row_total)))


def solution(mesh):
    placed = (
        P("rows", None),
        P("rows", None),
        P("rows", None),
        P("rows", "cols"),
        P("rows", "cols"),
    )
    return jax.shard_map(
        shards, mesh=mesh, in_specs=placed, out_specs=P("rows", "cols"), check_vma=False
    )
```

```python
import functools

import jax
import jax.numpy as jnp
from jax import lax
from jax.experimental import pallas as pl
from jax.experimental.pallas import tpu as pltpu
from jax.sharding import PartitionSpec as P

NX, NY, NZ, NH, NC = 4, 4, 2, 4, 2
BF = jnp.bfloat16
F32 = jnp.float32


def row_id(x, y, z):
    return (x % NX) * (NY * NZ) + (y % NY) * NZ + (z % NZ)


def get_rows(value, dx=0, dy=0, dz=0):
    pairs = [
        (row_id(x + dx, y + dy, z + dz), row_id(x, y, z))
        for x in range(NX)
        for y in range(NY)
        for z in range(NZ)
    ]
    return lax.ppermute(value, "rows", pairs)


def get_x(value, k):
    return get_rows(value, dx=k)


def get_y(value, k):
    return get_rows(value, dy=k)


def get_z(value):
    return get_rows(value, dz=1)


def get_cols(value, dh=0, dc=0):
    pairs = [
        (((h + dh) % NH) * NC + (c + dc) % NC, h * NC + c) for h in range(NH) for c in range(NC)
    ]
    return lax.ppermute(value, "cols", pairs)


def dot(a, b, contract=((1,), (0,))):
    return lax.dot_general(a, b, (contract, ((), ())), preferred_element_type=F32)


def pick(natural, size):
    j = lax.broadcasted_iota(jnp.int32, (size, size), 1)
    k = lax.broadcasted_iota(jnp.int32, (size, size), 0)
    return jnp.where(k == natural(j), 1.0, 0.0).astype(BF)


def ring_gather(block, get):
    half = block.shape[0] // 2
    one = get(block, 1)
    three = get(block, 3)
    two_a = get(one[:half], 1)
    two_b = get(three[half:], 3)
    return jnp.concatenate([block, one, two_a, two_b, three], axis=0)


def direct_gather(block, get):
    return jnp.concatenate([block] + [get(block, k) for k in (1, 2, 3)], axis=0)


def direct_reduce(parts, get):
    sent = parts.astype(BF)
    total = parts[0]
    for k in (1, 2, 3):
        total = total + get(sent[(4 - k) % 4], k).astype(F32)
    return total


def local_call(kernel, outs, args, scratch=(), flops=0, far=0, far_out=False):
    specs = [pl.BlockSpec(memory_space=pltpu.HBM)] * far
    specs += [pl.BlockSpec(memory_space=pltpu.VMEM)] * (len(args) - far)
    size = sum(a.size * a.dtype.itemsize for a in args)
    space = pltpu.HBM if far_out else pltpu.VMEM
    return pl.pallas_call(
        kernel,
        out_shape=outs,
        in_specs=specs,
        out_specs=jax.tree.map(lambda _: pl.BlockSpec(memory_space=space), outs),
        scratch_shapes=list(scratch),
        compiler_params=pltpu.CompilerParams(vmem_limit_bytes=(56 if far else 16) * 1024 * 1024),
        cost_estimate=pl.CostEstimate(flops=flops, bytes_accessed=size, transcendentals=0),
    )(*args)


def blocks():
    for k in range(4):
        for hs in range(NH):
            for ys in range(2):
                for xs in range(NX):
                    for zs in range(NZ):
                        dest = row_id(xs, (k % 2) * 2 + ys, zs)
                        yield k, hs * 256 + ys * 128 + xs * 32, zs, dest, (k // 2) * 128 + hs * 32


def cross_kernel(c0, c1, c2, c3, out):
    chunks = (c0, c1, c2, c3)
    for k, row, zs, dest, place in blocks():
        out[dest, place : place + 32, :] = chunks[k][row : row + 32, zs * 128 : (zs + 1) * 128]


def fit_kernel(p0, p1, p2, p3, sol, treat, cot, u, psi, got, sems, table, fitted):
    first = pltpu.make_async_copy(sol, got, sems.at[4])
    first.start()
    copies = [pltpu.make_async_copy(p, psi.at[k], sems.at[k]) for k, p in enumerate((p0, p1, p2, p3))]
    for copy in copies:
        copy.start()
    first.wait()
    tile = 256
    for k in range(4):
        for kk, row, zs, dest, place in blocks():
            if kk == k:
                table[k, row : row + 32, zs * 128 : (zs + 1) * 128] = got[
                    dest, place : place + 32, :
                ]
        copies[k].wait()

        @pl.loop(0, u.shape[0] // tile)
        def _(i):
            rows = pl.ds(pl.multiple_of(i * tile, tile), tile)
            part = jnp.dot(psi[k, rows, :], table[k], preferred_element_type=F32)
            if k == 0:
                fitted[rows, :] = part
            elif k < 3:
                fitted[rows, :] += part
            else:
                part = fitted[rows, :] + part
                u[rows, 0:128] = (cot[rows, :].astype(F32) - part[:, 128:256]).astype(BF)
                u[rows, 128:256] = (treat[rows, :].astype(F32) - part[:, 0:128]).astype(BF)


def grad_kernel(
    part, sol, sol_other, u_far, other_far, steep_far, hidden_far,
    own, one, two_top, two_bottom, three,
    got, left, steep, hidden, result, sems, out_sems, table, dpre,
):
    moves = [
        (sol.at[:, pl.ds(0, 128)], got.at[0]),
        (sol_other, got.at[1]),
        (u_far, left.at[0]),
        (other_far, left.at[1]),
        (steep_far, steep),
        (hidden_far, hidden),
    ]
    copies = [pltpu.make_async_copy(a, b, sems.at[i]) for i, (a, b) in enumerate(moves)]
    for copy in copies:
        copy.start()
    for side in range(2):
        copies[side].wait()
        for k, row, zs, dest, place in blocks():
            if k == part:
                table[side, row : row + 32, zs * 128 : (zs + 1) * 128] = got[
                    side, dest, place : place + 32, :
                ]
    for copy in copies[2:5]:
        copy.wait()
    tile = 256

    @pl.loop(0, dpre.shape[0] // tile)
    def _(i):
        rows = pl.ds(pl.multiple_of(i * tile, tile), tile)
        for lo in range(0, 1024, 256):
            terms = [
                lax.dot_general(
                    left[side, rows, :],
                    table[side, lo : lo + 256, :],
                    (((1,), (1,)), ((), ())),
                    preferred_element_type=F32,
                )
                for side in range(2)
            ]
            dpre[rows, lo : lo + 256] = (
                (terms[0] + terms[1]) * steep[rows, lo : lo + 256]
            ).astype(BF)

    copies[5].wait()
    sent = []
    for i, out in enumerate((two_top, two_bottom, one, three, own)):
        start = (512, 640, 256, 768, 0)[i]
        n = out.shape[0]
        for lo in range(0, 1024, 256):
            result[start : start + n, lo : lo + 256] = jnp.dot(
                hidden[start : start + n, :],
                dpre[:, lo : lo + 256],
                preferred_element_type=F32,
            ).astype(BF)
        copy = pltpu.make_async_copy(result.at[pl.ds(start, n)], out, out_sems.at[i])
        copy.start()
        sent.append(copy)
    for copy in sent:
        copy.wait()


def ring_reduce(pieces, get):
    own, one, two_top, two_bottom, three = pieces
    half = two_top.shape[0]
    from_three = get(two_top, 3)
    from_one = get(two_bottom, 1)
    one = jnp.concatenate([(one[:half].astype(F32) + from_three.astype(F32)).astype(BF), one[half:]])
    three = jnp.concatenate([three[:half], (three[half:].astype(F32) + from_one.astype(F32)).astype(BF)])
    return own.astype(F32) + get(one, 3).astype(F32) + get(three, 1).astype(F32)


def slope(v):
    sig = 0.5 * (1.0 + jnp.tanh(0.5 * v))
    return sig * (1.0 + v * (1.0 - sig))


def silu(v):
    return (0.5 * v) * (1.0 + jnp.tanh(0.5 * v))


def shards(hidden_in, w_out, inv_factor, treat_feat, section_cot):
    n_here = hidden_in.shape[0]
    row_total = n_here * lax.axis_size("rows")
    r = lax.axis_index("rows")
    c = lax.axis_index("cols")
    x, y, z = r // (NY * NZ), (r // NZ) % NY, r % NZ
    h, core = c // NC, c % NC

    def w_part(part):
        return jnp.concatenate(
            [
                lax.dynamic_slice(w_out, (0, (2 * hs + core) * 512 + part * 256), (32, 256))
                for hs in range(NH)
            ],
            axis=1,
        )

    w_half = jnp.stack([w_part(0), w_part(1)])
    w_pair = jnp.concatenate([w_half, get_z(w_half)], axis=1)
    w_pair, inv_factor = lax.optimization_barrier((w_pair, inv_factor))
    w_a = direct_gather(w_pair[0], get_x)
    w_b = direct_gather(w_pair[1], get_y)
    w_a, w_b, hidden_late = lax.optimization_barrier((w_a, w_b, hidden_in))
    w_a = ring_gather(w_a, get_y)
    w_b = ring_gather(w_b, get_x)

    def natural_a(j):
        ys, xs, zs, i = j // 256, (j // 64) % 4, (j // 32) % 2, j % 32
        return ((x + xs) % 4) * 256 + ((y + ys) % 4) * 64 + ((z + zs) % 2) * 32 + i

    def natural_b(j):
        xs, ys, zs, i = j // 256, (j // 64) % 4, (j // 32) % 2, j % 32
        return ((x + xs) % 4) * 256 + ((y + ys) % 4) * 64 + ((z + zs) % 2) * 32 + i

    h_a = dot(pick(natural_a, 1024), hidden_late, ((0,), (1,))).astype(BF)
    h_b = dot(pick(natural_b, 1024), hidden_late, ((0,), (1,))).astype(BF)

    l_half = lax.dynamic_slice_in_dim(inv_factor, core * 64, 64, 0).astype(BF)
    l_half = jnp.concatenate([l_half, get_z(l_half)], axis=0)

    def natural_l(j):
        xs, rc, hs, i = j // 256, (j // 128) % 2, (j // 32) % 4, j % 32
        return (hs * 2 + (core + rc) % 2) * 128 + ((x + xs) % 4) * 32 + i

    def l_cols(k):
        column = (y + 4 - k) % 4
        return jnp.concatenate(
            [
                lax.dynamic_slice(l_half, (0, (i * NY + column) * 128), (128, 128))
                for i in range(NH * NC)
            ],
            axis=1,
        )

    l_parts = [l_cols(k) for k in range(4)]
    w_a, w_b, l_parts = lax.optimization_barrier((w_a, w_b, l_parts))
    psi_a = silu(dot(h_a, w_a, ((0,), (0,)))).astype(BF)
    psi_a_other = get_cols(psi_a, dc=1)
    psi_b = silu(dot(h_b, w_b, ((0,), (0,)))).astype(BF)
    psi_b_other = get_cols(psi_b, dc=1)
    psis = [psi_a, psi_b, psi_a_other, psi_b_other]

    targets = jnp.concatenate([treat_feat, section_cot], axis=1)
    cross = [dot(p, targets, ((0,), (0,))).astype(BF) for p in psis]
    cross = local_call(cross_kernel, jax.ShapeDtypeStruct((32, 256, 128), BF), cross)
    cross, l_parts = lax.optimization_barrier((cross, l_parts))
    l_parts = jnp.stack([l_parts[0]] + [get_y(l_parts[k], k) for k in (1, 2, 3)])
    cross = lax.all_to_all(cross, "rows", 0, 0, tiled=True)
    l_block = jnp.concatenate([l_parts, get_cols(l_parts, dc=1)], axis=1).reshape(1024, 1024)
    l_block = dot(l_block, pick(natural_l, 1024)).astype(BF)
    cross, l_block = lax.optimization_barrier((cross, l_block))
    cross = jnp.sum(cross.astype(F32), axis=0).astype(BF)

    cross = direct_gather(cross, get_x)
    middle = dot(l_block, cross).reshape(4, 256, 128)
    middle = direct_reduce(middle, get_y).astype(BF)
    middle = direct_gather(middle, get_y)
    solved = dot(l_block, middle, ((0,), (0,))).reshape(4, 256, 128)
    solved = direct_reduce(solved, get_x).astype(BF)

    solved, w_a, w_b = lax.optimization_barrier((solved, w_a, w_b))
    slope_a = slope(dot(h_a, w_a, ((0,), (0,))))
    slope_b = slope(dot(h_b, w_b, ((0,), (0,))))
    sol = lax.all_to_all(jnp.broadcast_to(solved[None], (32, 256, 128)), "rows", 0, 0, tiled=True)
    sol, slope_a, slope_b = lax.optimization_barrier((sol, slope_a, slope_b))
    sol_other = get_cols(sol[:, 128:], dc=1)
    n_width = 2 * treat_feat.shape[1]
    u = local_call(
        fit_kernel,
        jax.ShapeDtypeStruct((n_here, n_width), BF),
        psis + [sol, treat_feat, section_cot],
        scratch=[
            pltpu.VMEM((4, n_here, 1024), BF),
            pltpu.VMEM((32, 256, 128), BF),
            pltpu.SemaphoreType.DMA((5,)),
            pltpu.VMEM((4, 1024, n_width), BF),
            pltpu.VMEM((n_here, n_width), F32),
        ],
        flops=2 * n_here * 4096 * n_width,
        far=5,
    )
    u_other = get_cols(u, dc=1)

    def grad_part(part, hidden, steep):
        return local_call(
            functools.partial(grad_kernel, part),
            [jax.ShapeDtypeStruct((n, 1024), BF) for n in (256, 256, 128, 128, 256)],
            [sol, sol_other, u, u_other, steep, hidden],
            scratch=[
                pltpu.VMEM((2, 32, 128, 128), BF),
                pltpu.VMEM((2, n_here, n_width), BF),
                pltpu.VMEM((n_here, 1024), F32),
                pltpu.VMEM((1024, n_here), BF),
                pltpu.VMEM((1024, 1024), BF),
                pltpu.SemaphoreType.DMA((6,)),
                pltpu.SemaphoreType.DMA((5,)),
                pltpu.VMEM((2, 1024, n_width), BF),
                pltpu.VMEM((n_here, 1024), BF),
            ],
            flops=2 * n_here * 1024 * 1536,
            far=6,
            far_out=True,
        )

    grad_a = ring_reduce(grad_part(0, h_b, slope_a), get_x).reshape(4, 64, 1024)
    grad_b = ring_reduce(grad_part(1, h_a, slope_b), get_y).reshape(4, 64, 1024)
    grad_a = direct_reduce(grad_a, get_y)
    grad_b = direct_reduce(grad_b, get_x)
    kept = jnp.stack([grad_a[:32], grad_b[:32]])
    sent = jnp.stack([grad_a[32:], grad_b[32:]]).astype(BF)
    grad = (kept + get_z(sent).astype(F32)).reshape(2, 32, NH, 256)

    def for_h(k):
        return lax.dynamic_index_in_dim(grad, (h + 4 - k) % 4, 2, keepdims=False)

    total = for_h(0)
    for k in (1, 2, 3):
        total = total + get_cols(for_h(k).astype(BF), dh=k).astype(F32)
    total = jnp.concatenate([total[0], total[1]], axis=1)
    return total * (1.0 / jnp.sqrt(jnp.float32(row_total)))


def solution(mesh):
    placed = (
        P("rows", None),
        P("rows", None),
        P("rows", None),
        P("rows", "cols"),
        P("rows", "cols"),
    )
    return jax.shard_map(
        shards, mesh=mesh, in_specs=placed, out_specs=P("rows", "cols"), check_vma=False
    )
```

```python
import functools

import jax
import jax.numpy as jnp
from jax import lax
from jax.experimental import pallas as pl
from jax.experimental.pallas import tpu as pltpu
from jax.sharding import PartitionSpec as P

NX, NY, NZ, NH, NC = 4, 4, 2, 4, 2
BF = jnp.bfloat16
F32 = jnp.float32


def row_id(x, y, z):
    return (x % NX) * (NY * NZ) + (y % NY) * NZ + (z % NZ)


def get_rows(value, dx=0, dy=0, dz=0):
    pairs = [
        (row_id(x + dx, y + dy, z + dz), row_id(x, y, z))
        for x in range(NX)
        for y in range(NY)
        for z in range(NZ)
    ]
    return lax.ppermute(value, "rows", pairs)


def get_x(value, k):
    return get_rows(value, dx=k)


def get_y(value, k):
    return get_rows(value, dy=k)


def get_z(value):
    return get_rows(value, dz=1)


def get_cols(value, dh=0, dc=0):
    pairs = [
        (((h + dh) % NH) * NC + (c + dc) % NC, h * NC + c) for h in range(NH) for c in range(NC)
    ]
    return lax.ppermute(value, "cols", pairs)


def dot(a, b, contract=((1,), (0,))):
    return lax.dot_general(a, b, (contract, ((), ())), preferred_element_type=F32)


def pick(natural, size):
    j = lax.broadcasted_iota(jnp.int32, (size, size), 1)
    k = lax.broadcasted_iota(jnp.int32, (size, size), 0)
    return jnp.where(k == natural(j), 1.0, 0.0).astype(BF)


def ring_gather(block, get):
    half = block.shape[0] // 2
    one = get(block, 1)
    three = get(block, 3)
    two_a = get(one[:half], 1)
    two_b = get(three[half:], 3)
    return jnp.concatenate([block, one, two_a, two_b, three], axis=0)


def direct_gather(block, get):
    return jnp.concatenate([block] + [get(block, k) for k in (1, 2, 3)], axis=0)


def direct_reduce(parts, get):
    sent = parts.astype(BF)
    total = parts[0]
    for k in (1, 2, 3):
        total = total + get(sent[(4 - k) % 4], k).astype(F32)
    return total


def local_call(kernel, outs, args, scratch=(), flops=0, far=0, far_out=False):
    specs = [pl.BlockSpec(memory_space=pltpu.HBM)] * far
    specs += [pl.BlockSpec(memory_space=pltpu.VMEM)] * (len(args) - far)
    size = sum(a.size * a.dtype.itemsize for a in args)
    space = pltpu.HBM if far_out else pltpu.VMEM
    return pl.pallas_call(
        kernel,
        out_shape=outs,
        in_specs=specs,
        out_specs=jax.tree.map(lambda _: pl.BlockSpec(memory_space=space), outs),
        scratch_shapes=list(scratch),
        compiler_params=pltpu.CompilerParams(vmem_limit_bytes=(56 if far else 16) * 1024 * 1024),
        cost_estimate=pl.CostEstimate(flops=flops, bytes_accessed=size, transcendentals=0),
    )(*args)


def blocks():
    for k in range(4):
        for hs in range(NH):
            for ys in range(2):
                for xs in range(NX):
                    for zs in range(NZ):
                        dest = row_id(xs, (k % 2) * 2 + ys, zs)
                        yield k, hs * 256 + ys * 128 + xs * 32, zs, dest, (k // 2) * 128 + hs * 32


def cross_kernel(c0, c1, c2, c3, out):
    chunks = (c0, c1, c2, c3)
    for k, row, zs, dest, place in blocks():
        out[dest, place : place + 32, :] = chunks[k][row : row + 32, zs * 128 : (zs + 1) * 128]


def fit_kernel(p0, p1, p2, p3, sol, treat, cot, u, psi, got, sems, table, fitted):
    first = pltpu.make_async_copy(sol, got, sems.at[4])
    first.start()
    copies = [pltpu.make_async_copy(p, psi.at[k], sems.at[k]) for k, p in enumerate((p0, p1, p2, p3))]
    for copy in copies:
        copy.start()
    first.wait()
    tile = 256
    for k in range(4):
        for kk, row, zs, dest, place in blocks():
            if kk == k:
                table[k, row : row + 32, zs * 128 : (zs + 1) * 128] = got[
                    dest, place : place + 32, :
                ]
        copies[k].wait()

        @pl.loop(0, u.shape[0] // tile)
        def _(i):
            rows = pl.ds(pl.multiple_of(i * tile, tile), tile)
            part = jnp.dot(psi[k, rows, :], table[k], preferred_element_type=F32)
            if k == 0:
                fitted[rows, :] = part
            elif k < 3:
                fitted[rows, :] += part
            else:
                part = fitted[rows, :] + part
                u[rows, 0:128] = (cot[rows, :].astype(F32) - part[:, 128:256]).astype(BF)
                u[rows, 128:256] = (treat[rows, :].astype(F32) - part[:, 0:128]).astype(BF)


def grad_kernel(
    part, sol, sol_other, u_far, other_far, steep_far, hidden_far,
    own, one_top, one_bottom, two_top, two_bottom, three_top, three_bottom,
    got, left, steep, hidden, result, sems, out_sems, table, dpre,
):
    moves = [
        (sol.at[:, pl.ds(0, 128)], got.at[0]),
        (sol_other, got.at[1]),
        (u_far, left.at[0]),
        (other_far, left.at[1]),
        (steep_far, steep),
        (hidden_far, hidden),
    ]
    copies = [pltpu.make_async_copy(a, b, sems.at[i]) for i, (a, b) in enumerate(moves)]
    for copy in copies:
        copy.start()
    for side in range(2):
        copies[side].wait()
        for k, row, zs, dest, place in blocks():
            if k == part:
                table[side, row : row + 32, zs * 128 : (zs + 1) * 128] = got[
                    side, dest, place : place + 32, :
                ]
    for copy in copies[2:5]:
        copy.wait()
    tile = 256

    @pl.loop(0, dpre.shape[0] // tile)
    def _(i):
        rows = pl.ds(pl.multiple_of(i * tile, tile), tile)
        for lo in range(0, 1024, 256):
            terms = [
                lax.dot_general(
                    left[side, rows, :],
                    table[side, lo : lo + 256, :],
                    (((1,), (1,)), ((), ())),
                    preferred_element_type=F32,
                )
                for side in range(2)
            ]
            dpre[rows, lo : lo + 256] = (
                (terms[0] + terms[1]) * steep[rows, lo : lo + 256]
            ).astype(BF)

    copies[5].wait()
    sent = []
    groups = (
        (512, (two_top, two_bottom)),
        (256, (one_top, one_bottom)),
        (768, (three_top, three_bottom)),
        (0, (own,)),
    )
    for first, outs in groups:
        for lo in range(0, 1024, 256):
            result[first : first + 256, lo : lo + 256] = jnp.dot(
                hidden[first : first + 256, :],
                dpre[:, lo : lo + 256],
                preferred_element_type=F32,
            ).astype(BF)
        for out in outs:
            n = out.shape[0]
            copy = pltpu.make_async_copy(result.at[pl.ds(first, n)], out, out_sems.at[len(sent)])
            copy.start()
            sent.append(copy)
            first += n
    for copy in sent:
        copy.wait()


def ring_reduce(pieces, get):
    own, one_top, one_bottom, two_top, two_bottom, three_top, three_bottom = pieces
    from_three = get(two_top, 3)
    from_one = get(two_bottom, 1)
    one_top = (one_top.astype(F32) + from_three.astype(F32)).astype(BF)
    three_bottom = (three_bottom.astype(F32) + from_one.astype(F32)).astype(BF)
    one = jnp.concatenate([one_top, one_bottom])
    three = jnp.concatenate([three_top, three_bottom])
    return own.astype(F32) + get(one, 3).astype(F32) + get(three, 1).astype(F32)


def slope(v):
    sig = 0.5 * (1.0 + jnp.tanh(0.5 * v))
    return sig * (1.0 + v * (1.0 - sig))


def silu(v):
    return (0.5 * v) * (1.0 + jnp.tanh(0.5 * v))


def shards(hidden_in, w_out, inv_factor, treat_feat, section_cot):
    n_here = hidden_in.shape[0]
    row_total = n_here * lax.axis_size("rows")
    r = lax.axis_index("rows")
    c = lax.axis_index("cols")
    x, y, z = r // (NY * NZ), (r // NZ) % NY, r % NZ
    h, core = c // NC, c % NC

    def w_part(part):
        return jnp.concatenate(
            [
                lax.dynamic_slice(w_out, (0, (2 * hs + core) * 512 + part * 256), (32, 256))
                for hs in range(NH)
            ],
            axis=1,
        )

    w_half = jnp.stack([w_part(0), w_part(1)])
    w_pair = jnp.concatenate([w_half, get_z(w_half)], axis=1)
    w_pair, inv_factor = lax.optimization_barrier((w_pair, inv_factor))
    w_a = direct_gather(w_pair[0], get_x)
    w_b = direct_gather(w_pair[1], get_y)
    w_a, w_b, hidden_late = lax.optimization_barrier((w_a, w_b, hidden_in))
    w_a = ring_gather(w_a, get_y)
    w_b = ring_gather(w_b, get_x)

    def natural_a(j):
        ys, xs, zs, i = j // 256, (j // 64) % 4, (j // 32) % 2, j % 32
        return ((x + xs) % 4) * 256 + ((y + ys) % 4) * 64 + ((z + zs) % 2) * 32 + i

    def natural_b(j):
        xs, ys, zs, i = j // 256, (j // 64) % 4, (j // 32) % 2, j % 32
        return ((x + xs) % 4) * 256 + ((y + ys) % 4) * 64 + ((z + zs) % 2) * 32 + i

    h_a = dot(pick(natural_a, 1024), hidden_late, ((0,), (1,))).astype(BF)
    h_b = dot(pick(natural_b, 1024), hidden_late, ((0,), (1,))).astype(BF)

    l_half = lax.dynamic_slice_in_dim(inv_factor, core * 64, 64, 0).astype(BF)
    l_half = jnp.concatenate([l_half, get_z(l_half)], axis=0)

    def natural_l(j):
        xs, rc, hs, i = j // 256, (j // 128) % 2, (j // 32) % 4, j % 32
        return (hs * 2 + (core + rc) % 2) * 128 + ((x + xs) % 4) * 32 + i

    def l_cols(k):
        column = (y + 4 - k) % 4
        return jnp.concatenate(
            [
                lax.dynamic_slice(l_half, (0, (i * NY + column) * 128), (128, 128))
                for i in range(NH * NC)
            ],
            axis=1,
        )

    l_parts = [l_cols(k) for k in range(4)]
    w_a, w_b, l_parts = lax.optimization_barrier((w_a, w_b, l_parts))
    psi_a = silu(dot(h_a, w_a, ((0,), (0,)))).astype(BF)
    psi_a_other = get_cols(psi_a, dc=1)
    psi_a, l_parts = lax.optimization_barrier((psi_a, l_parts))
    l_parts = [l_parts[0]] + [get_y(l_parts[k], k) for k in (1, 2, 3)]
    psi_b = silu(dot(h_b, w_b, ((0,), (0,)))).astype(BF)
    psi_b_other = get_cols(psi_b, dc=1)
    psis = [psi_a, psi_b, psi_a_other, psi_b_other]

    targets = jnp.concatenate([treat_feat, section_cot], axis=1)
    cross = [dot(p, targets, ((0,), (0,))).astype(BF) for p in psis]
    cross = local_call(cross_kernel, jax.ShapeDtypeStruct((32, 256, 128), BF), cross)
    cross, l_parts = lax.optimization_barrier((cross, l_parts))
    l_parts = jnp.stack(l_parts)
    cross = lax.all_to_all(cross, "rows", 0, 0, tiled=True)
    l_block = jnp.concatenate([l_parts, get_cols(l_parts, dc=1)], axis=1).reshape(1024, 1024)
    l_block = dot(l_block, pick(natural_l, 1024)).astype(BF)
    cross, l_block = lax.optimization_barrier((cross, l_block))
    cross = jnp.sum(cross.astype(F32), axis=0).astype(BF)

    cross = direct_gather(cross, get_x)
    middle = dot(l_block, cross).reshape(4, 256, 128)
    middle = direct_reduce(middle, get_y).astype(BF)
    middle = direct_gather(middle, get_y)
    solved = dot(l_block, middle, ((0,), (0,))).reshape(4, 256, 128)
    solved = direct_reduce(solved, get_x).astype(BF)

    solved, w_a, w_b = lax.optimization_barrier((solved, w_a, w_b))
    slope_a = slope(dot(h_a, w_a, ((0,), (0,))))
    slope_b = slope(dot(h_b, w_b, ((0,), (0,))))
    sol = lax.all_to_all(jnp.broadcast_to(solved[None], (32, 256, 128)), "rows", 0, 0, tiled=True)
    sol, slope_a, slope_b = lax.optimization_barrier((sol, slope_a, slope_b))
    sol_other = get_cols(sol[:, 128:], dc=1)
    n_width = 2 * treat_feat.shape[1]
    u = local_call(
        fit_kernel,
        jax.ShapeDtypeStruct((n_here, n_width), BF),
        psis + [sol, treat_feat, section_cot],
        scratch=[
            pltpu.VMEM((4, n_here, 1024), BF),
            pltpu.VMEM((32, 256, 128), BF),
            pltpu.SemaphoreType.DMA((5,)),
            pltpu.VMEM((4, 1024, n_width), BF),
            pltpu.VMEM((n_here, n_width), F32),
        ],
        flops=2 * n_here * 4096 * n_width,
        far=5,
    )
    u_other = get_cols(u, dc=1)

    def grad_part(part, hidden, steep):
        return local_call(
            functools.partial(grad_kernel, part),
            [jax.ShapeDtypeStruct((n, 1024), BF) for n in (256, 128, 128, 128, 128, 128, 128)],
            [sol, sol_other, u, u_other, steep, hidden],
            scratch=[
                pltpu.VMEM((2, 32, 128, 128), BF),
                pltpu.VMEM((2, n_here, n_width), BF),
                pltpu.VMEM((n_here, 1024), F32),
                pltpu.VMEM((1024, n_here), BF),
                pltpu.VMEM((1024, 1024), BF),
                pltpu.SemaphoreType.DMA((6,)),
                pltpu.SemaphoreType.DMA((7,)),
                pltpu.VMEM((2, 1024, n_width), BF),
                pltpu.VMEM((n_here, 1024), BF),
            ],
            flops=2 * n_here * 1024 * 1536,
            far=6,
            far_out=True,
        )

    grad_a = ring_reduce(grad_part(0, h_b, slope_a), get_x).reshape(4, 64, 1024)
    grad_b = ring_reduce(grad_part(1, h_a, slope_b), get_y).reshape(4, 64, 1024)
    grad_a = direct_reduce(grad_a, get_y)
    grad_b = direct_reduce(grad_b, get_x)
    kept = jnp.stack([grad_a[:32], grad_b[:32]])
    sent = jnp.stack([grad_a[32:], grad_b[32:]]).astype(BF)
    grad = (kept + get_z(sent).astype(F32)).reshape(2, 32, NH, 256)

    def for_h(k):
        return lax.dynamic_index_in_dim(grad, (h + 4 - k) % 4, 2, keepdims=False)

    total = for_h(0)
    for k in (1, 2, 3):
        total = total + get_cols(for_h(k).astype(BF), dh=k).astype(F32)
    total = jnp.concatenate([total[0], total[1]], axis=1)
    return total * (1.0 / jnp.sqrt(jnp.float32(row_total)))


def solution(mesh):
    placed = (
        P("rows", None),
        P("rows", None),
        P("rows", None),
        P("rows", "cols"),
        P("rows", "cols"),
    )
    return jax.shard_map(
        shards, mesh=mesh, in_specs=placed, out_specs=P("rows", "cols"), check_vma=False
    )
```
